512 devices in a mesh: dom: 32 (over z, y_hi), span: 16 (over x, y_lo, core).
Axes of the slice: x: 4, y: 4 (y_hi: 2, y_lo: 2; y = y_hi * 2 + y_lo), z: 16, core: 2. Of those that a mesh axis runs over, the one named last changes fastest.
Arguments:
- entities: bfloat16 [32768, 256], P('dom'), may hold values from -2.5 to 2.5
- operators: bfloat16 [64, 256, 256], P('span'), may hold values from -0.375 to 0.375
- left_rows: int32 [3, 32, 16, 512], P(None, 'dom', 'span'), may hold values from 0 to 1023
- right_rows: int32 [3, 32, 16, 512], P(None, 'dom', 'span'), may hold values from 0 to 1023
- negatives: int32 [3, 32, 16, 1024], P(None, 'dom', 'span'), may hold values from 0 to 1023
- counts: int32 [3, 32, 16, 64], P(None, 'dom', 'span'), may hold values from 1 to 8, as said below
Outputs:
- entity_grad: float32 [32768, 256], P(('dom', 'span'))
- relation_grad: float32 [64, 256, 256], P('span', 'dom')
The draws below stay inside these ranges and needn't reach their ends.
Inputs may be any that keep to these rules, and one draw needn't show every extreme that they name: `counts`: in every bucket step and partition one relation has all 8 slots live in every group's list.
All inputs are finite; a program needn't handle non-finite values.
Results may differ from the reference program's by a relative error of at most 0.0021.
Values may be sent and summed in bfloat16 or wider, within the bound.
No kernel may reach another device: no remote copies, remote signals or barrier semaphores. Data moves between devices by JAX's collectives and lax.ppermute only.
A program may use at most 64 MiB of HBM per device.

```python
import jax
import jax.numpy as jnp
from jax import lax

D = 256
R = 64
NEG = 1024
CAP = 8
STEPS = 3
PART_ROWS = 1024
SLOTS = 512
ENT = 32768
N_DOM = 32
N_SPAN = 16


def draw_counts(key, part):
    key = jax.random.fold_in(key, 11)
    level_key, count_key, full_key = jax.random.split(key, 3)
    levels = jax.random.randint(level_key, (STEPS, N_DOM, N_SPAN, 1), CAP // 2, CAP + 1)
    random_counts = jax.random.randint(count_key, (STEPS, N_DOM, N_SPAN, R), 1, levels + 1)
    full_relation = jax.random.randint(full_key, (STEPS, N_DOM, 1, 1), 0, R)
    relation_ids = jnp.arange(R, dtype=jnp.int32).reshape(1, 1, 1, R)
    return jnp.where(relation_ids == full_relation, CAP, random_counts).astype(jnp.int32)


def with_ends(result, own_key, low, largest):
    extent = result.shape
    index_at = [jax.random.randint(jax.random.fold_in(own_key, axis), (), 0, extent[axis]) for axis in range(len(extent))]
    result = result.at[tuple(index_at)].set(low)
    longest = extent.index(max(extent))
    index_at[longest] = (index_at[longest] + 1) % extent[longest]
    return result.at[tuple(index_at)].set(largest)


def block_scale(key, shape, cuts, low, top_value):
    level, own = 1.0, jax.random.fold_in(key, 6)
    for axis_at, blocks in cuts:
        heights = jnp.exp(jax.random.uniform(jax.random.fold_in(own, axis_at), (blocks,), jnp.float32, low / len(cuts), top_value / len(cuts)))
        level = level * jnp.repeat(heights, shape[axis_at] // blocks).reshape([-1 if axis == axis_at else 1 for axis in range(len(shape))])
    return level


def bell_draw(rng, dims, deviation, limit, pieces=(), kind=jnp.bfloat16):
    drawn = jax.random.normal(rng, dims, jnp.float32) * deviation
    if len(pieces) > 0:
        drawn = block_scale(rng, dims, pieces, -0.22, 0.18) * drawn
    return jnp.clip(drawn, min=-limit, max=limit).astype(kind)


def setup_inputs(seed: int = 0) -> dict:
    key_of = jax.random.split(jax.random.key(seed), 7)
    entities = bell_draw(key_of[0], (ENT, D), 0.35, 2.5, ((0, 32),))
    operators = bell_draw(key_of[1], (R, D, D), D ** -0.5, 0.375, ((0, 16),))
    left_rows = with_ends(jax.random.randint(key_of[2], (STEPS, N_DOM, N_SPAN, SLOTS), 0, PART_ROWS), jax.random.fold_in(key_of[2], 1), 0, PART_ROWS - 1).astype(jnp.int32)
    right_rows = with_ends(jax.random.randint(key_of[3], (STEPS, N_DOM, N_SPAN, SLOTS), 0, PART_ROWS), jax.random.fold_in(key_of[3], 1), 0, PART_ROWS - 1).astype(jnp.int32)
    negatives = with_ends(jax.random.randint(key_of[4], (STEPS, N_DOM, N_SPAN, NEG), 0, PART_ROWS), jax.random.fold_in(key_of[4], 1), 0, PART_ROWS - 1).astype(jnp.int32)
    counts = draw_counts(jax.random.fold_in(key_of[6], 71), 0)
    return dict(entities=entities, operators=operators, left_rows=left_rows, right_rows=right_rows, negatives=negatives, counts=counts)


def live_slots(count_row):
    return (count_row[:, None] > jnp.arange(CAP, dtype=jnp.int32)[None, :]).astype(jnp.float32).reshape(-1)


def reference(entities, operators, left_rows, right_rows, negatives, counts):
    neg_scale = float(NEG) ** -0.5
    operators_wide = operators.astype(jnp.float32)

    def visit_bucket(totals, position):
        ent_grad, rel_grad = totals
        bucket = position // (N_DOM * N_SPAN)
        remainder = position % (N_DOM * N_SPAN)
        partition = remainder // N_SPAN
        group_id = remainder % N_SPAN
        right_part = (partition + bucket) % N_DOM
        left_index = left_rows[bucket, partition, group_id] + partition * PART_ROWS
        right_index = right_rows[bucket, partition, group_id] + right_part * PART_ROWS
        negative_index = negatives[bucket, partition, group_id] + right_part * PART_ROWS
        live_mask = live_slots(counts[bucket, partition, group_id])
        left_vecs = entities[left_index]
        right_vecs = entities[right_index]
        negative_vecs = entities[negative_index]
        queries = jnp.einsum("rkd,rde->rke", left_vecs.reshape(R, CAP, D).astype(jnp.float32), operators_wide)
        queries = queries.reshape(SLOTS, D).astype(jnp.bfloat16)
        queries_wide = queries.astype(jnp.float32)
        positive = jnp.sum(queries_wide * right_vecs.astype(jnp.float32), axis=1)
        scores = jnp.dot(queries, negative_vecs.T, preferred_element_type=jnp.float32)
        pos_grad = -live_mask * jax.nn.sigmoid(-positive)
        neg_grad = (live_mask[:, None] * jax.nn.sigmoid(scores) * neg_scale).astype(jnp.bfloat16)
        query_grad = pos_grad[:, None] * right_vecs.astype(jnp.float32) + jnp.dot(neg_grad, negative_vecs, preferred_element_type=jnp.float32)
        query_grad = query_grad.astype(jnp.bfloat16)
        grad_blocks = query_grad.reshape(R, CAP, D).astype(jnp.float32)
        left_grad = jnp.einsum("rke,rde->rkd", grad_blocks, operators_wide).reshape(SLOTS, D).astype(jnp.bfloat16)
        rel_grad = rel_grad + jnp.einsum("rkd,rke->rde", left_vecs.reshape(R, CAP, D).astype(jnp.float32), grad_blocks)
        negative_rows = jnp.dot(neg_grad.T, queries, preferred_element_type=jnp.float32)
        ent_grad = ent_grad.at[left_index].add(left_grad.astype(jnp.float32))
        ent_grad = ent_grad.at[right_index].add(pos_grad[:, None] * queries_wide)
        ent_grad = ent_grad.at[negative_index].add(negative_rows)
        return (ent_grad, rel_grad), None

    initial = (jnp.zeros((ENT, D), jnp.float32), jnp.zeros((R, D, D), jnp.float32))
    totals, _ = lax.scan(visit_bucket, initial, jnp.arange(STEPS * N_DOM * N_SPAN, dtype=jnp.int32))
    return totals[0], totals[1]
```

```python
import functools

import jax
import jax.numpy as jnp
from jax import lax
from jax.experimental import pallas as pl
from jax.experimental.pallas import tpu as pltpu
from jax.sharding import PartitionSpec as P

BF = jnp.bfloat16
F32 = jnp.float32
NT = (((1,), (1,)), ((), ()))
TN = (((0,), (0,)), ((), ()))
VMEM = pl.BlockSpec(memory_space=pltpu.VMEM)
SMEM = pl.BlockSpec(memory_space=pltpu.SMEM)


def dot(a, b, dims=(((1,), (0,)), ((), ()))):
    return lax.dot_general(a, b, dims, preferred_element_type=F32)


def passed_along(value, axis, steps):
    count = lax.axis_size(axis)
    pairs = [(source, (source + steps) % count) for source in range(count)]
    return lax.ppermute(value, axis, pairs)


def exchanged(value, axis):
    return lax.all_to_all(value, axis, split_axis=0, concat_axis=0, tiled=True)


def iota(shape, axis):
    return lax.broadcasted_iota(jnp.int32, shape, axis)


def pack_kernel(buckets, groups, neg_ref, pair_ref, count_ref, out_ref):
    neg_count = neg_ref.shape[1]
    hist_rows = 8 * buckets
    for s in range(buckets):
        row = neg_ref[s : s + 1, :]
        high = (iota((16, neg_count), 0) == (row >> 7)).astype(F32).astype(BF)
        low = (iota((128, neg_count), 0) == (row & 127)).astype(F32).astype(BF)
        hist = dot(high, low, NT)[:8].astype(jnp.int32)
        for d in range(groups):
            out_ref[d, 8 * s : 8 * s + 8, :] = hist
    lines = pair_ref.shape[0] // buckets
    rest = jnp.zeros((8 - 2 * buckets, 128), jnp.int32)
    counts = count_ref[...]
    counts = jnp.concatenate([counts, jnp.zeros((buckets, 128 - counts.shape[1]), jnp.int32)], 1)
    for line in range(lines):
        pairs = [pair_ref[lines * s + line : lines * s + line + 1, :] for s in range(buckets)]
        block = jnp.concatenate(pairs + [counts, rest], 0)
        for d in range(line * groups // lines, (line + 1) * groups // lines):
            out_ref[d, hist_rows : hist_rows + 8, :] = block


def bucket_kernel(
    buckets, neg_scale, me_ref, x_ref, *refs
):
    slab_refs = refs[:buckets]
    ops_ref = refs[buckets]
    ent_ref, rel_ref = refs[buckets + 1 : buckets + 3]
    left_acc, rel_acc, ohl_ref, ng_ref, whi_ref, wlo_ref, mult_ref, rows_ref = refs[buckets + 3 :]
    rel_own, width, _ = ops_ref.shape
    groups = x_ref.shape[0]
    part_rows = slab_refs[0].shape[0]
    slots = rel_own * 128
    chunk = 128
    chunks = part_rows // chunk
    hist_rows = 8 * buckets
    share = part_rows // groups
    me = me_ref[0]

    lane_row = iota((128, slots), 0)
    lane = iota((128, slots), 1)
    relation, slot = lane >> 7, lane & 7
    per_line = 128 // (8 * rel_own)
    pick_slot = (lane_row == (me % per_line) * (8 * rel_own) + relation * 8 + slot)
    pick_slot = pick_slot.astype(F32).astype(BF)
    pick_count = (lane_row == me * rel_own + relation).astype(F32).astype(BF)
    lane = iota((groups, slots), 1)
    own_group = iota((groups, slots), 0) == ((lane >> 3) & (groups - 1))
    slot_row = iota((1, slots), 1) & 7

    def own(values):
        return jnp.sum(jnp.where(own_group, values, 0.0), axis=0, keepdims=True)

    def narrow(values):
        return values.astype(F32).astype(BF)

    for step, s in enumerate(list(range(1, buckets)) + [0]):
        slab = slab_refs[s]
        pair = x_ref[:, hist_rows + s, :]
        left, right = pair & 65535, pair >> 16
        parts = [left >> 5, left & 31, right >> 5, right & 31]
        parts = dot(narrow(jnp.concatenate(parts, 0)), pick_slot)
        parts = [own(parts[groups * q : groups * (q + 1)]) for q in range(4)]
        left_row = (parts[0] * 32.0 + parts[1]).astype(jnp.int32)
        right_row = (parts[2] * 32.0 + parts[3]).astype(jnp.int32)
        count_row = own(dot(narrow(x_ref[:, hist_rows + buckets + s, :]), pick_count))
        live = (count_row.astype(jnp.int32) > slot_row).astype(F32)

        for a in range(8):
            hist = x_ref[:, 8 * s + a, :].astype(F32)
            hist = jnp.broadcast_to(hist[:, None, :], (groups, 8, 128)).reshape(128, 128)
            mult_ref[128 * a : 128 * (a + 1), :] = hist.T

        def left_hot(n, carry):
            at = pl.multiple_of(n * chunk, chunk)
            rows = iota((chunk, slots), 0) + n * chunk
            ohl_ref[pl.ds(at, chunk), :] = (rows == left_row).astype(F32).astype(BF)
            return carry

        lax.fori_loop(0, chunks, left_hot, 0)
        left_t = dot(slab_refs[0][...], ohl_ref[...], TN).astype(BF)
        query_t = jnp.concatenate(
            [dot(ops_ref[i], left_t[:, 128 * i : 128 * (i + 1)], TN) for i in range(rel_own)], 1
        ).astype(BF)

        def score(n, positive):
            at = pl.multiple_of(n * chunk, chunk)
            scores = dot(slab[pl.ds(at, chunk), :], query_t)
            sig = 0.5 * jnp.tanh(0.5 * scores) + 0.5
            ng_ref[pl.ds(at, chunk), :] = (live * sig * neg_scale).astype(BF)
            hit = (iota((chunk, slots), 0) + n * chunk) == right_row
            return positive + jnp.sum(jnp.where(hit, scores, 0.0), axis=0, keepdims=True)

        positive = lax.fori_loop(0, chunks, score, jnp.zeros((1, slots), F32))
        pos_grad = -live * jax.nn.sigmoid(-positive)

        def weigh(n, carry):
            at = pl.multiple_of(n * chunk, chunk)
            mult = mult_ref[pl.ds(at, chunk), :]
            mult = jnp.concatenate([mult] * rel_own, 1)
            hit = (iota((chunk, slots), 0) + n * chunk) == right_row
            weight = ng_ref[pl.ds(at, chunk), :].astype(F32) * mult
            weight = weight + jnp.where(hit, pos_grad, 0.0)
            high = weight.astype(BF)
            whi_ref[pl.ds(at, chunk), :] = high
            wlo_ref[pl.ds(at, chunk), :] = (weight - high.astype(F32)).astype(BF)
            return carry

        lax.fori_loop(0, chunks, weigh, 0)
        whole = slab[...]
        qgrad_t = (dot(whole, whi_ref[...], TN) + dot(whole, wlo_ref[...], TN)).astype(BF)
        rows_ref[...] = dot(whi_ref[...], query_t, NT) + dot(wlo_ref[...], query_t, NT)
        lgrad_t = jnp.concatenate(
            [dot(ops_ref[i], qgrad_t[:, 128 * i : 128 * (i + 1)]) for i in range(rel_own)], 1
        ).astype(BF)
        left_rows = dot(ohl_ref[...], lgrad_t, NT)
        left_acc[...] = left_rows if step == 0 else left_acc[...] + left_rows
        for i in range(rel_own):
            cols = slice(128 * i, 128 * (i + 1))
            outer = dot(left_t[:, cols], qgrad_t[:, cols], NT)
            rel_acc[i] = outer if step == 0 else rel_acc[i] + outer
        for d in range(groups):
            block = rows_ref[share * d : share * (d + 1), :]
            if s == 0:
                block = block + left_acc[share * d : share * (d + 1), :]
            ent_ref[d, share * s : share * (s + 1), :] = block.astype(BF)

    doms, held, _ = rel_ref.shape
    held = held // rel_own
    for d in range(doms):
        block = [rel_acc[i, held * d : held * (d + 1), :] for i in range(rel_own)]
        rel_ref[d] = jnp.concatenate(block, 0).astype(BF)


def shards(entities, operators, left_rows, right_rows, negatives, counts):
    buckets = left_rows.shape[0]
    slot_count = left_rows.shape[-1]
    neg_count = negatives.shape[-1]
    groups = lax.axis_size("span")
    doms = lax.axis_size("dom")
    rel_own = operators.shape[0]
    relations = rel_own * groups
    part_rows, width = entities.shape
    neg_scale = float(neg_count) ** (-0.5)
    share = part_rows // groups
    slots = rel_own * 128

    pair = (left_rows + (right_rows << 16)).reshape(buckets * slot_count // 128, 128)
    packed = pl.pallas_call(
        functools.partial(pack_kernel, buckets, groups),
        out_shape=jax.ShapeDtypeStruct((groups, 8 * buckets + 8, 128), jnp.int32),
        in_specs=[VMEM] * 3,
        out_specs=VMEM,
        name="pack_lists",
    )(negatives.reshape(buckets, neg_count), pair, counts.reshape(buckets, relations))
    received = exchanged(packed, "span")
    slabs = [entities] + [passed_along(entities, "dom", -s) for s in range(1, buckets)]

    me = lax.axis_index("span").astype(jnp.int32).reshape(1)
    ent_parts, rel_parts = pl.pallas_call(
        functools.partial(bucket_kernel, buckets, neg_scale),
        out_shape=(
            jax.ShapeDtypeStruct((groups, buckets * share, width), BF),
            jax.ShapeDtypeStruct((doms, rel_own * width // doms, width), BF),
        ),
        in_specs=[SMEM] + [VMEM] * (buckets + 2),
        out_specs=(VMEM, VMEM),
        scratch_shapes=[
            pltpu.VMEM((part_rows, width), F32),
            pltpu.VMEM((rel_own, width, width), F32),
            pltpu.VMEM((part_rows, slots), BF),
            pltpu.VMEM((part_rows, slots), BF),
            pltpu.VMEM((part_rows, slots), BF),
            pltpu.VMEM((part_rows, slots), BF),
            pltpu.VMEM((part_rows, 128), F32),
            pltpu.VMEM((part_rows, width), F32),
        ],
        compiler_params=pltpu.CompilerParams(vmem_limit_bytes=40 * 1024 * 1024),
        cost_estimate=pl.CostEstimate(
            flops=6_200_000_000, bytes_accessed=6_000_000, transcendentals=1_600_000
        ),
        name="buckets",
    )(me, received, *slabs, operators)

    ent_shares = jnp.sum(exchanged(ent_parts, "span").astype(F32), axis=0)
    entity_share = ent_shares[:share]
    for s in range(1, buckets):
        entity_share = entity_share + passed_along(ent_shares[share * s : share * (s + 1)], "dom", s)
    rel_share = jnp.sum(exchanged(rel_parts, "dom").astype(F32), axis=0)
    return (entity_share, rel_share.reshape(rel_own, width // doms, width))


def solution(mesh):
    in_specs = (
        P("dom", None),
        P("span", None, None),
        P(None, "dom", "span", None),
        P(None, "dom", "span", None),
        P(None, "dom", "span", None),
        P(None, "dom", "span", None),
    )
    out_specs = (P(("dom", "span"), None), P("span", "dom", None))
    return jax.shard_map(shards, mesh=mesh, in_specs=in_specs, out_specs=out_specs, check_vma=False)
```

```python
import functools

import jax
import jax.numpy as jnp
from jax import lax
from jax.experimental import pallas as pl
from jax.experimental.pallas import tpu as pltpu
from jax.sharding import PartitionSpec as P

BF = jnp.bfloat16
F32 = jnp.float32
NT = (((1,), (1,)), ((), ()))
TN = (((0,), (0,)), ((), ()))
VMEM = pl.BlockSpec(memory_space=pltpu.VMEM)
SMEM = pl.BlockSpec(memory_space=pltpu.SMEM)


def dot(a, b, dims=(((1,), (0,)), ((), ()))):
    return lax.dot_general(a, b, dims, preferred_element_type=F32)


def passed_along(value, axis, steps):
    count = lax.axis_size(axis)
    pairs = [(source, (source + steps) % count) for source in range(count)]
    return lax.ppermute(value, axis, pairs)


def exchanged(value, axis):
    return lax.all_to_all(value, axis, split_axis=0, concat_axis=0, tiled=True)


def iota(shape, axis):
    return lax.broadcasted_iota(jnp.int32, shape, axis)


def pack_kernel(buckets, groups, neg_ref, left_ref, right_ref, count_ref, out_ref):
    hist_rows = 8 * buckets
    for s in range(buckets):
        high, low = [], []
        for q in range(neg_ref.shape[1]):
            row = neg_ref[s, q : q + 1, :]
            high.append((iota((16, 128), 0) == (row >> 7)).astype(F32).astype(BF))
            low.append((iota((128, 128), 0) == (row & 127)).astype(F32).astype(BF))
        hist = dot(jnp.concatenate(high, 1), jnp.concatenate(low, 1), NT)[:8].astype(jnp.int32)
        for d in range(groups):
            out_ref[d, 8 * s : 8 * s + 8, :] = hist
    lines = left_ref.shape[1]
    rest = jnp.zeros((8 - 2 * buckets, 128), jnp.int32)
    counts = [count_ref[s] for s in range(buckets)]
    counts = jnp.concatenate(counts, 0)
    counts = jnp.concatenate([counts, jnp.zeros((buckets, 128 - counts.shape[1]), jnp.int32)], 1)
    for line in range(lines):
        pairs = [
            left_ref[s, line : line + 1, :] + (right_ref[s, line : line + 1, :] << 16)
            for s in range(buckets)
        ]
        block = jnp.concatenate(pairs + [counts, rest], 0)
        for d in range(line * groups // lines, (line + 1) * groups // lines):
            out_ref[d, hist_rows : hist_rows + 8, :] = block


def one_hot(rows, at, shape):
    return ((iota(shape, 0) + at) == rows).astype(F32).astype(BF)


def spread_counts(hist, groups, mult_ref, a):
    hist = jnp.broadcast_to(hist[:, None, :], (groups, 8, 128)).reshape(128, 128)
    mult_ref[128 * a : 128 * (a + 1), :] = hist.T


def forward_kernel(buckets, neg_scale, me_ref, x_ref, *refs):
    slab_refs = refs[:buckets]
    ops_ref = refs[buckets]
    rel_ref, qg_ref, lrow_ref = refs[buckets + 1 : buckets + 4]
    pk_refs = refs[buckets + 4 : 2 * buckets + 4]
    rel_acc, et0_ref, et_ref, oh_ref, whi_ref, wlo_ref, mult_ref = refs[2 * buckets + 4 :]
    rel_own, width, _ = ops_ref.shape
    groups = x_ref.shape[0]
    part_rows = slab_refs[0].shape[0]
    slots = rel_own * 128
    chunk = 256
    chunks = part_rows // chunk
    hist_rows = 8 * buckets
    me = me_ref[0]

    lane_row = iota((128, slots), 0)
    lane = iota((128, slots), 1)
    relation, slot = lane >> 7, lane & 7
    per_line = 128 // (8 * rel_own)
    pick_slot = (lane_row == (me % per_line) * (8 * rel_own) + relation * 8 + slot)
    pick_slot = pick_slot.astype(F32).astype(BF)
    pick_count = (lane_row == me * rel_own + relation).astype(F32).astype(BF)
    lane = iota((groups, slots), 1)
    own_group = iota((groups, slots), 0) == ((lane >> 3) & (groups - 1))
    slot_row = iota((1, slots), 1) & 7

    def own(values):
        return jnp.sum(jnp.where(own_group, values, 0.0), axis=0, keepdims=True)

    def narrow(values):
        return values.astype(F32).astype(BF)

    et0_ref[...] = slab_refs[0][...].T
    for s in range(buckets):
        slab, pk = slab_refs[s], pk_refs[s]
        pair = x_ref[:, hist_rows + s, :]
        left, right = pair & 65535, pair >> 16
        parts = [left >> 5, left & 31, right >> 5, right & 31]
        parts = dot(narrow(jnp.concatenate(parts, 0)), pick_slot)
        parts = [own(parts[groups * q : groups * (q + 1)]) for q in range(4)]
        left_row = (parts[0] * 32.0 + parts[1]).astype(jnp.int32)
        right_row = (parts[2] * 32.0 + parts[3]).astype(jnp.int32)
        count_row = own(dot(narrow(x_ref[:, hist_rows + buckets + s, :]), pick_count))
        live = (count_row.astype(jnp.int32) > slot_row).astype(F32)
        lrow_ref[s : s + 1, :] = left_row

        highs, lows = [], []
        for a in range(8):
            hist = x_ref[:, 8 * s + a, :]
            highs.append(hist >> 5)
            lows.append(hist & 31)
            spread_counts(hist.astype(F32), groups, mult_ref, a)
        for q, group in enumerate([highs[:4], highs[4:], lows[:4], lows[4:]]):
            at = width + 16 * q
            pk[at : at + 16, :] = narrow(jnp.concatenate(group, 1))

        if s == 0:
            slab_t = et0_ref
        else:
            et_ref[...] = slab[...].T
            slab_t = et_ref

        def left_hot(n, carry):
            at = pl.multiple_of(n * chunk, chunk)
            oh_ref[pl.ds(at, chunk), :] = one_hot(left_row, n * chunk, (chunk, slots))
            return carry

        def right_hot(n, carry):
            at = pl.multiple_of(n * chunk, chunk)
            oh_ref[pl.ds(at, chunk), :] = one_hot(right_row, n * chunk, (chunk, slots))
            return carry

        lax.fori_loop(0, chunks, left_hot, 0)
        left_t = dot(et0_ref[...], oh_ref[...]).astype(BF)
        query_t = jnp.concatenate(
            [dot(ops_ref[i], left_t[:, 128 * i : 128 * (i + 1)], TN) for i in range(rel_own)], 1
        ).astype(BF)
        pk[0:width, :] = query_t
        half_t = query_t * 0.5
        lax.fori_loop(0, chunks, right_hot, 0)
        right_t = dot(slab_t[...], oh_ref[...])
        positive = jnp.sum(query_t.astype(F32) * right_t, axis=0, keepdims=True)
        pos_grad = -live * jax.nn.sigmoid(-positive)
        pos_high = pos_grad.astype(BF)
        pos_low = (pos_grad - pos_high.astype(F32)).astype(BF)
        misc = [narrow(parts[2]), narrow(parts[3]), narrow(live), pos_high, pos_low]
        misc = [row.astype(F32) for row in misc] + [jnp.zeros((11, slots), F32)]
        pk[width + 64 : width + 80, :] = jnp.concatenate(misc, 0).astype(BF)
        factor = live * (0.5 * neg_scale)

        def weigh(n, carry):
            at = pl.multiple_of(n * chunk, chunk)
            level = jnp.tanh(dot(slab[pl.ds(at, chunk), :], half_t))
            ngrad = (level * factor + factor).astype(BF).astype(F32)
            mult = mult_ref[pl.ds(at, chunk), :]
            weight = ngrad * jnp.concatenate([mult] * rel_own, 1)
            high = weight.astype(BF)
            whi_ref[pl.ds(at, chunk), :] = high
            wlo_ref[pl.ds(at, chunk), :] = (weight - high.astype(F32)).astype(BF)
            return carry

        lax.fori_loop(0, chunks, weigh, 0)
        qgrad_t = dot(slab_t[...], whi_ref[...]) + dot(slab_t[...], wlo_ref[...])
        qgrad_t = (qgrad_t + right_t * pos_grad).astype(BF)
        qg_ref[s] = qgrad_t
        for i in range(rel_own):
            cols = slice(128 * i, 128 * (i + 1))
            outer = dot(left_t[:, cols], qgrad_t[:, cols], NT)
            rel_acc[i] = outer if s == 0 else rel_acc[i] + outer

    doms, held, _ = rel_ref.shape
    held = held // rel_own
    for d in range(doms):
        block = [rel_acc[i, held * d : held * (d + 1), :] for i in range(rel_own)]
        rel_ref[d] = jnp.concatenate(block, 0).astype(BF)


def entity_kernel(buckets, neg_scale, groups, me_ref, slab_ref, ops_ref, qg_ref, lrow_ref, *refs):
    pk_refs = refs[:buckets]
    keep_ref, send_ref, rows_ref, mult_ref = refs[buckets:]
    me = me_ref[0]
    rel_own, width, _ = ops_ref.shape
    part_rows = slab_ref.shape[0]
    slots = rel_own * 128
    chunk = 256
    chunks = part_rows // chunk
    share = part_rows // groups
    for s in range(buckets):
        pk = pk_refs[s]
        left_row = lrow_ref[s : s + 1, :]
        qgrad_t = qg_ref[s]
        lgrad_t = jnp.concatenate(
            [dot(ops_ref[i], qgrad_t[:, 128 * i : 128 * (i + 1)]) for i in range(rel_own)], 1
        ).astype(BF)
        hist = pk[width : width + 64, :].astype(F32)
        hist = hist[:32] * 32.0 + hist[32:]
        for a in range(8):
            cols = slice(128 * (a % 4), 128 * (a % 4 + 1))
            spread_counts(hist[16 * (a // 4) : 16 * (a // 4 + 1), cols], groups, mult_ref, a)
        misc = pk[width + 64 : width + 80, :].astype(F32)
        right_row = (misc[0:1] * 32.0 + misc[1:2]).astype(jnp.int32)
        factor = misc[2:3] * (0.5 * neg_scale)
        pos_grad = misc[3:4] + misc[4:5]
        query_t = pk[0:width, :]
        half_t = query_t * 0.5

        def weigh(n, carry):
            at = pl.multiple_of(n * chunk, chunk)
            level = jnp.tanh(dot(slab_ref[pl.ds(at, chunk), :], half_t))
            ngrad = (level * factor + factor).astype(BF).astype(F32)
            mult = mult_ref[pl.ds(at, chunk), :]
            hit = (iota((chunk, slots), 0) + n * chunk) == right_row
            weight = ngrad * jnp.concatenate([mult] * rel_own, 1) + jnp.where(hit, pos_grad, 0.0)
            high = weight.astype(BF)
            low = (weight - high.astype(F32)).astype(BF)
            hot = one_hot(left_row, n * chunk, (chunk, slots))
            rows = dot(high, query_t, NT) + dot(low, query_t, NT) + dot(hot, lgrad_t, NT)
            rows_ref[pl.ds(at, chunk), :] = rows if s == 0 else rows_ref[pl.ds(at, chunk), :] + rows
            return carry

        lax.fori_loop(0, chunks, weigh, 0)
    core, y, x = me & 1, (me >> 1) & 1, me >> 2
    pair, mirror = (x ^ (x >> 1)) & 1, x >> 1
    for n in range(groups):
        to_pair, to_mirror = pair ^ ((n >> 2) & 1), mirror ^ ((n >> 1) & 1)
        to_x = to_pair + to_mirror * (3 - 2 * to_pair)
        to = 4 * to_x + 2 * (y ^ (n & 1)) + (core ^ (n >> 3))
        block = rows_ref[pl.ds(pl.multiple_of(to * share, share), share), :]
        half = groups // 2
        if n < half:
            keep_ref[n] = block
        else:
            send_ref[n - half] = block


def shards(entities, operators, left_rows, right_rows, negatives, counts):
    buckets = left_rows.shape[0]
    slot_count = left_rows.shape[-1]
    neg_count = negatives.shape[-1]
    groups = lax.axis_size("span")
    doms = lax.axis_size("dom")
    rel_own = operators.shape[0]
    relations = rel_own * groups
    part_rows, width = entities.shape
    neg_scale = float(neg_count) ** (-0.5)
    share = part_rows // groups
    slots = rel_own * 128
    limit = pltpu.CompilerParams(vmem_limit_bytes=40 * 1024 * 1024)

    packed = pl.pallas_call(
        functools.partial(pack_kernel, buckets, groups),
        out_shape=jax.ShapeDtypeStruct((groups, 8 * buckets + 8, 128), jnp.int32),
        in_specs=[VMEM] * 4,
        out_specs=VMEM,
        name="pack_lists",
    )(
        negatives.reshape(buckets, neg_count // 128, 128),
        left_rows.reshape(buckets, slot_count // 128, 128),
        right_rows.reshape(buckets, slot_count // 128, 128),
        counts.reshape(buckets, 1, relations),
    )
    received = exchanged(packed, "span")
    slabs = [entities] + [passed_along(entities, "dom", -s) for s in range(1, buckets)]

    me = lax.axis_index("span").astype(jnp.int32).reshape(1)
    pack = jax.ShapeDtypeStruct((width + 80, slots), BF)
    wide = pltpu.VMEM((part_rows, slots), BF)
    rel_parts, qgrads, lrows, *packs = pl.pallas_call(
        functools.partial(forward_kernel, buckets, neg_scale),
        out_shape=[
            jax.ShapeDtypeStruct((doms, rel_own * width // doms, width), BF),
            jax.ShapeDtypeStruct((buckets, width, slots), BF),
            jax.ShapeDtypeStruct((8, slots), jnp.int32),
        ]
        + [pack] * buckets,
        in_specs=[SMEM] + [VMEM] * (buckets + 2),
        out_specs=[VMEM] * (buckets + 3),
        scratch_shapes=[
            pltpu.VMEM((rel_own, width, width), F32),
            pltpu.VMEM((width, part_rows), BF),
            pltpu.VMEM((width, part_rows), BF),
            wide,
            wide,
            wide,
            pltpu.VMEM((part_rows, 128), F32),
        ],
        compiler_params=limit,
        cost_estimate=pl.CostEstimate(
            flops=4_400_000_000, bytes_accessed=4_000_000, transcendentals=1_600_000
        ),
        name="query_gradients",
    )(me, received, *slabs, operators)
    packs = [packs[0]] + [passed_along(packs[s], "dom", s) for s in range(1, buckets)]
    rel_arrived = exchanged(rel_parts, "dom")

    half_parts = jax.ShapeDtypeStruct((groups // 2, share, width), F32)
    keep, send = pl.pallas_call(
        functools.partial(entity_kernel, buckets, neg_scale, groups),
        out_shape=(half_parts, half_parts),
        in_specs=[SMEM] + [VMEM] * (buckets + 4),
        out_specs=(VMEM, VMEM),
        scratch_shapes=[
            pltpu.VMEM((part_rows, width), F32),
            pltpu.VMEM((part_rows, 128), F32),
        ],
        compiler_params=limit,
        cost_estimate=pl.CostEstimate(
            flops=4_000_000_000, bytes_accessed=3_000_000, transcendentals=1_600_000
        ),
        name="entity_gradients",
    )(me, entities, operators, qgrads, lrows, *packs)
    for partner in (1, 4, 12, 2):
        got = lax.ppermute(send, "span", [(i, i ^ partner) for i in range(groups)])
        half = keep.shape[0] // 2
        if half:
            send, keep = keep[half:] + got[half:], keep[:half] + got[:half]
        else:
            entity_share = (keep + got).reshape(share, width)
    rel_share = jnp.sum(rel_arrived.astype(F32), axis=0)
    return (entity_share, rel_share.reshape(rel_own, width // doms, width))


def solution(mesh):
    in_specs = (
        P("dom", None),
        P("span", None, None),
        P(None, "dom", "span", None),
        P(None, "dom", "span", None),
        P(None, "dom", "span", None),
        P(None, "dom", "span", None),
    )
    out_specs = (P(("dom", "span"), None), P("span", "dom", None))
    return jax.shard_map(shards, mesh=mesh, in_specs=in_specs, out_specs=out_specs, check_vma=False)
```

```python
import functools

import jax
import jax.numpy as jnp
from jax import lax
from jax.experimental import pallas as pl
from jax.experimental.pallas import tpu as pltpu
from jax.sharding import PartitionSpec as P

BF = jnp.bfloat16
F32 = jnp.float32
NT = (((1,), (1,)), ((), ()))
TN = (((0,), (0,)), ((), ()))
VMEM = pl.BlockSpec(memory_space=pltpu.VMEM)
SMEM = pl.BlockSpec(memory_space=pltpu.SMEM)


def dot(a, b, dims=(((1,), (0,)), ((), ()))):
    return lax.dot_general(a, b, dims, preferred_element_type=F32)


def passed_along(value, axis, steps):
    count = lax.axis_size(axis)
    pairs = [(source, (source + steps) % count) for source in range(count)]
    return lax.ppermute(value, axis, pairs)


def exchanged(value, axis):
    return lax.all_to_all(value, axis, split_axis=0, concat_axis=0, tiled=True)


def iota(shape, axis):
    return lax.broadcasted_iota(jnp.int32, shape, axis)


def pack_kernel(buckets, groups, neg_ref, left_ref, right_ref, count_ref, out_ref):
    hist_rows = 8 * buckets
    for s in range(buckets):
        high, low = [], []
        for q in range(neg_ref.shape[1]):
            row = neg_ref[s, q : q + 1, :]
            high.append((iota((16, 128), 0) == (row >> 7)).astype(F32).astype(BF))
            low.append((iota((128, 128), 0) == (row & 127)).astype(F32).astype(BF))
        hist = dot(jnp.concatenate(high, 1), jnp.concatenate(low, 1), NT)[:8].astype(jnp.int32)
        for d in range(groups):
            out_ref[d, 8 * s : 8 * s + 8, :] = hist
    lines = left_ref.shape[1]
    rest = jnp.zeros((8 - 2 * buckets, 128), jnp.int32)
    counts = [count_ref[s] for s in range(buckets)]
    counts = jnp.concatenate(counts, 0)
    counts = jnp.concatenate([counts, jnp.zeros((buckets, 128 - counts.shape[1]), jnp.int32)], 1)
    for line in range(lines):
        pairs = [
            left_ref[s, line : line + 1, :] + (right_ref[s, line : line + 1, :] << 16)
            for s in range(buckets)
        ]
        block = jnp.concatenate(pairs + [counts, rest], 0)
        for d in range(line * groups // lines, (line + 1) * groups // lines):
            out_ref[d, hist_rows : hist_rows + 8, :] = block


def loop(n, step, carry):
    for i in range(n):
        carry = step(i, carry)
    return carry


def one_hot(rows, at, shape):
    return ((iota(shape, 0) + at) == rows).astype(F32).astype(BF)


def spread_counts(hist, groups, mult_ref, a):
    hist = jnp.broadcast_to(hist[:, None, :], (groups, 8, 128)).reshape(128, 128)
    mult_ref[128 * a : 128 * (a + 1), :] = hist.T


def forward_kernel(buckets, which, neg_scale, me_ref, x_ref, *refs):
    first = which[0] == 0
    many = len(which)
    slab_refs, ops_ref = refs[:many], refs[many]
    refs = refs[many + 1 :]
    if first:
        rel_acc, et0_ref = refs[:2]
        refs = refs[2:]
    else:
        et0_ref, sum_ref, rel_ref = refs[:3]
        refs = refs[3:]
    qg_ref, lrow_ref = refs[:2]
    pk_refs, refs = refs[2 : many + 2], refs[many + 2 :]
    oh_ref, whi_ref, wlo_ref, mult_ref = refs[:4]
    if not first:
        rel_acc, et_ref = refs[4:]
    rel_own, width, _ = ops_ref.shape
    groups = x_ref.shape[0]
    part_rows = slab_refs[0].shape[0]
    slots = rel_own * 128
    chunk = 256
    chunks = part_rows // chunk
    hist_rows = 8 * buckets
    me = me_ref[0]

    lane_row = iota((128, slots), 0)
    lane = iota((128, slots), 1)
    relation, slot = lane >> 7, lane & 7
    per_line = 128 // (8 * rel_own)
    pick_slot = (lane_row == (me % per_line) * (8 * rel_own) + relation * 8 + slot)
    pick_slot = pick_slot.astype(F32).astype(BF)
    pick_count = (lane_row == me * rel_own + relation).astype(F32).astype(BF)
    lane = iota((groups, slots), 1)
    own_group = iota((groups, slots), 0) == ((lane >> 3) & (groups - 1))
    slot_row = iota((1, slots), 1) & 7

    def own(values):
        return jnp.sum(jnp.where(own_group, values, 0.0), axis=0, keepdims=True)

    def narrow(values):
        return values.astype(F32).astype(BF)

    for at_call, s in enumerate(which):
        slab, pk = slab_refs[at_call], pk_refs[at_call]
        pair = x_ref[:, hist_rows + s, :]
        left, right = pair & 65535, pair >> 16
        parts = [left >> 5, left & 31, right >> 5, right & 31]
        parts = dot(narrow(jnp.concatenate(parts, 0)), pick_slot)
        parts = [own(parts[groups * q : groups * (q + 1)]) for q in range(4)]
        left_row = (parts[0] * 32.0 + parts[1]).astype(jnp.int32)
        right_row = (parts[2] * 32.0 + parts[3]).astype(jnp.int32)
        count_row = own(dot(narrow(x_ref[:, hist_rows + buckets + s, :]), pick_count))
        live = (count_row.astype(jnp.int32) > slot_row).astype(F32)
        lrow_ref[at_call : at_call + 1, :] = left_row

        highs, lows = [], []
        for a in range(8):
            hist = x_ref[:, 8 * s + a, :]
            highs.append(hist >> 5)
            lows.append(hist & 31)
            spread_counts(hist.astype(F32), groups, mult_ref, a)
        for q, group in enumerate([highs[:4], highs[4:], lows[:4], lows[4:]]):
            at = width + 16 * q
            pk[at : at + 16, :] = narrow(jnp.concatenate(group, 1))

        slab_t = et0_ref if first else et_ref
        slab_t[...] = slab[...].T

        def left_hot(n, carry):
            at = n * chunk
            oh_ref[pl.ds(at, chunk), :] = one_hot(left_row, n * chunk, (chunk, slots))
            return carry

        def right_hot(n, carry):
            at = n * chunk
            oh_ref[pl.ds(at, chunk), :] = one_hot(right_row, n * chunk, (chunk, slots))
            return carry

        loop(chunks, left_hot, 0)
        left_t = dot(et0_ref[...], oh_ref[...]).astype(BF)
        query_t = jnp.concatenate(
            [dot(ops_ref[i], left_t[:, 128 * i : 128 * (i + 1)], TN) for i in range(rel_own)], 1
        ).astype(BF)
        pk[0:width, :] = query_t
        half_t = query_t * 0.5
        loop(chunks, right_hot, 0)
        right_t = dot(slab_t[...], oh_ref[...])
        positive = jnp.sum(query_t.astype(F32) * right_t, axis=0, keepdims=True)
        pos_grad = -live * jax.nn.sigmoid(-positive)
        pos_high = pos_grad.astype(BF)
        pos_low = (pos_grad - pos_high.astype(F32)).astype(BF)
        misc = [narrow(parts[2]), narrow(parts[3]), narrow(live), pos_high, pos_low]
        misc = [row.astype(F32) for row in misc] + [jnp.zeros((11, slots), F32)]
        pk[width + 64 : width + 80, :] = jnp.concatenate(misc, 0).astype(BF)
        factor = live * (0.5 * neg_scale)

        def weigh(n, carry):
            at = n * chunk
            level = jnp.tanh(dot(slab[pl.ds(at, chunk), :], half_t))
            ngrad = (level * factor + factor).astype(BF).astype(F32)
            mult = mult_ref[pl.ds(at, chunk), :]
            weight = ngrad * jnp.concatenate([mult] * rel_own, 1)
            high = weight.astype(BF)
            whi_ref[pl.ds(at, chunk), :] = high
            wlo_ref[pl.ds(at, chunk), :] = (weight - high.astype(F32)).astype(BF)
            return carry

        loop(chunks, weigh, 0)
        qgrad_t = dot(slab_t[...], whi_ref[...]) + dot(slab_t[...], wlo_ref[...])
        qgrad_t = (qgrad_t + right_t * pos_grad).astype(BF)
        qg_ref[at_call] = qgrad_t
        for i in range(rel_own):
            cols = slice(128 * i, 128 * (i + 1))
            outer = dot(left_t[:, cols], qgrad_t[:, cols], NT)
            if first:
                rel_acc[i] = outer
            elif at_call == 0:
                rel_acc[i] = sum_ref[i] + outer
            else:
                rel_acc[i] = rel_acc[i] + outer

    if first:
        return
    doms, held, _ = rel_ref.shape
    held = held // rel_own
    for d in range(doms):
        block = [rel_acc[i, held * d : held * (d + 1), :] for i in range(rel_own)]
        rel_ref[d] = jnp.concatenate(block, 0).astype(BF)


def entity_kernel(buckets, neg_scale, groups, me_ref, slab_ref, ops_ref, *refs):
    qg0_ref, lrow0_ref, qg_ref, lrow_ref = refs[:4]
    pk_refs = refs[4 : 4 + buckets]
    keep_ref, send_ref, rows_ref, mult_ref = refs[4 + buckets :]
    me = me_ref[0]
    rel_own, width, _ = ops_ref.shape
    part_rows = slab_ref.shape[0]
    slots = rel_own * 128
    chunk = 256
    chunks = part_rows // chunk
    share = part_rows // groups
    for s in range(buckets):
        pk = pk_refs[s]
        left_row = lrow_ref[s - 1 : s, :] if s else lrow0_ref[0:1, :]
        qgrad_t = qg_ref[s - 1] if s else qg0_ref[0]
        lgrad_t = jnp.concatenate(
            [dot(ops_ref[i], qgrad_t[:, 128 * i : 128 * (i + 1)]) for i in range(rel_own)], 1
        ).astype(BF)
        hist = pk[width : width + 64, :].astype(F32)
        hist = hist[:32] * 32.0 + hist[32:]
        for a in range(8):
            cols = slice(128 * (a % 4), 128 * (a % 4 + 1))
            spread_counts(hist[16 * (a // 4) : 16 * (a // 4 + 1), cols], groups, mult_ref, a)
        misc = pk[width + 64 : width + 80, :].astype(F32)
        right_row = (misc[0:1] * 32.0 + misc[1:2]).astype(jnp.int32)
        factor = misc[2:3] * (0.5 * neg_scale)
        pos_grad = misc[3:4] + misc[4:5]
        query_t = pk[0:width, :]
        half_t = query_t * 0.5

        def weigh(n, carry):
            at = n * chunk
            level = jnp.tanh(dot(slab_ref[pl.ds(at, chunk), :], half_t))
            ngrad = (level * factor + factor).astype(BF).astype(F32)
            mult = mult_ref[pl.ds(at, chunk), :]
            hit = (iota((chunk, slots), 0) + n * chunk) == right_row
            weight = ngrad * jnp.concatenate([mult] * rel_own, 1) + jnp.where(hit, pos_grad, 0.0)
            high = weight.astype(BF)
            low = (weight - high.astype(F32)).astype(BF)
            hot = one_hot(left_row, n * chunk, (chunk, slots))
            rows = dot(high, query_t, NT) + dot(low, query_t, NT) + dot(hot, lgrad_t, NT)
            rows_ref[pl.ds(at, chunk), :] = rows if s == 0 else rows_ref[pl.ds(at, chunk), :] + rows
            return carry

        loop(chunks, weigh, 0)
    for n in range(groups):
        to = me ^ (((n >> 1) & 3) * 4 + (n & 1) * 2 + (n >> 3))
        block = rows_ref[pl.ds(pl.multiple_of(to * share, share), share), :]
        half = groups // 2
        if n < half:
            keep_ref[n] = block
        else:
            send_ref[n - half] = block


def shards(entities, operators, left_rows, right_rows, negatives, counts):
    buckets = left_rows.shape[0]
    slot_count = left_rows.shape[-1]
    neg_count = negatives.shape[-1]
    groups = lax.axis_size("span")
    doms = lax.axis_size("dom")
    rel_own = operators.shape[0]
    relations = rel_own * groups
    part_rows, width = entities.shape
    neg_scale = float(neg_count) ** (-0.5)
    share = part_rows // groups
    slots = rel_own * 128
    limit = pltpu.CompilerParams(vmem_limit_bytes=24 * 1024 * 1024)

    packed = pl.pallas_call(
        functools.partial(pack_kernel, buckets, groups),
        out_shape=jax.ShapeDtypeStruct((groups, 8 * buckets + 8, 128), jnp.int32),
        in_specs=[VMEM] * 4,
        out_specs=VMEM,
        name="pack_lists",
    )(
        negatives.reshape(buckets, neg_count // 128, 128),
        left_rows.reshape(buckets, slot_count // 128, 128),
        right_rows.reshape(buckets, slot_count // 128, 128),
        counts.reshape(buckets, 1, relations),
    )
    received = exchanged(packed, "span")
    slabs = [entities] + [passed_along(entities, "dom", -s) for s in range(1, buckets)]

    me = lax.axis_index("span").astype(jnp.int32).reshape(1)
    wide = pltpu.VMEM((part_rows, slots), BF)
    scratch = [wide, wide, wide, pltpu.VMEM((part_rows, 128), F32)]

    def packs_of(many):
        return [
            jax.ShapeDtypeStruct((many, width, slots), BF),
            jax.ShapeDtypeStruct((8, slots), jnp.int32),
        ] + [jax.ShapeDtypeStruct((width + 80, slots), BF)] * many

    rel_sum, slab_t, qg_own, lrow_own, pack_own = pl.pallas_call(
        functools.partial(forward_kernel, buckets, (0,), neg_scale),
        out_shape=[
            jax.ShapeDtypeStruct((rel_own, width, width), F32),
            jax.ShapeDtypeStruct((width, part_rows), BF),
        ]
        + packs_of(1),
        in_specs=[SMEM] + [VMEM] * 3,
        out_specs=[VMEM] * 5,
        scratch_shapes=scratch,
        compiler_params=limit,
        cost_estimate=pl.CostEstimate(
            flops=1_400_000_000, bytes_accessed=2_000_000, transcendentals=500_000
        ),
        name="own_bucket",
    )(me, received, entities, operators)
    others = tuple(range(1, buckets))
    rel_parts, qg_other, lrow_other, *packs = pl.pallas_call(
        functools.partial(forward_kernel, buckets, others, neg_scale),
        out_shape=[jax.ShapeDtypeStruct((doms, rel_own * width // doms, width), BF)]
        + packs_of(buckets - 1),
        in_specs=[SMEM] + [VMEM] * (buckets + 3),
        out_specs=[VMEM] * (buckets + 2),
        scratch_shapes=scratch
        + [pltpu.VMEM((rel_own, width, width), F32), pltpu.VMEM((width, part_rows), BF)],
        compiler_params=limit,
        cost_estimate=pl.CostEstimate(
            flops=3_000_000_000, bytes_accessed=3_000_000, transcendentals=1_100_000
        ),
        name="other_buckets",
    )(me, received, *slabs[1:], operators, slab_t, rel_sum)
    packs = [pack_own] + [passed_along(packs[s - 1], "dom", s) for s in others]
    rel_arrived = exchanged(rel_parts, "dom")

    half_parts = jax.ShapeDtypeStruct((groups // 2, share, width), F32)
    keep, send = pl.pallas_call(
        functools.partial(entity_kernel, buckets, neg_scale, groups),
        out_shape=(half_parts, half_parts),
        in_specs=[SMEM] + [VMEM] * (buckets + 6),
        out_specs=(VMEM, VMEM),
        scratch_shapes=[
            pltpu.VMEM((part_rows, width), F32),
            pltpu.VMEM((part_rows, 128), F32),
        ],
        compiler_params=limit,
        cost_estimate=pl.CostEstimate(
            flops=4_000_000_000, bytes_accessed=3_000_000, transcendentals=1_600_000
        ),
        name="entity_gradients",
    )(me, entities, operators, qg_own, lrow_own, qg_other, lrow_other, *packs)

    def swapped(value, bits):
        return lax.ppermute(value, "span", [(i, i ^ bits) for i in range(groups)])

    total = keep + swapped(send, 1)
    total = total.reshape(4, 2, share, width)
    got = [swapped(total[x].astype(BF), 4 * x) for x in (1, 2, 3)]
    total = total[0] + sum(part.astype(F32) for part in got)
    entity_share = total[0] + swapped(total[1], 2)
    rel_share = jnp.sum(rel_arrived.astype(F32), axis=0)
    return (entity_share, rel_share.reshape(rel_own, width // doms, width))


def solution(mesh):
    in_specs = (
        P("dom", None),
        P("span", None, None),
        P(None, "dom", "span", None),
        P(None, "dom", "span", None),
        P(None, "dom", "span", None),
        P(None, "dom", "span", None),
    )
    out_specs = (P(("dom", "span"), None), P("span", "dom", None))
    return jax.shard_map(shards, mesh=mesh, in_specs=in_specs, out_specs=out_specs, check_vma=False)
```

```python
import functools

import jax
import jax.numpy as jnp
from jax import lax
from jax.experimental import pallas as pl
from jax.experimental.pallas import tpu as pltpu
from jax.sharding import PartitionSpec as P

BF = jnp.bfloat16
F32 = jnp.float32
NT = (((1,), (1,)), ((), ()))
TN = (((0,), (0,)), ((), ()))
VMEM = pl.BlockSpec(memory_space=pltpu.VMEM)
SMEM = pl.BlockSpec(memory_space=pltpu.SMEM)
HBM = pl.BlockSpec(memory_space=pltpu.HBM)


def dot(a, b, dims=(((1,), (0,)), ((), ()))):
    return lax.dot_general(a, b, dims, preferred_element_type=F32)


def shifted(value, step, other):
    doms, groups = lax.axis_size("dom"), lax.axis_size("span")
    pairs = []
    for p in range(doms):
        for c in range(groups):
            to = (p + (other if c & 1 else step)) % doms
            pairs.append((p * groups + c, to * groups + c))
    return lax.ppermute(value, ("dom", "span"), pairs)


def swapped(value, bits):
    groups = lax.axis_size("span")
    return lax.ppermute(value, "span", [(i, i ^ bits) for i in range(groups)])


def exchanged(value, axis):
    return lax.all_to_all(value, axis, split_axis=0, concat_axis=0, tiled=True)


def iota(shape, axis):
    return lax.broadcasted_iota(jnp.int32, shape, axis)


def pack_kernel(buckets, groups, neg_ref, left_ref, right_ref, count_ref, out_ref):
    hist_rows = 8 * buckets
    for s in range(buckets):
        high, low = [], []
        for q in range(neg_ref.shape[1]):
            row = neg_ref[s, q : q + 1, :]
            high.append((iota((16, 128), 0) == (row >> 7)).astype(F32).astype(BF))
            low.append((iota((128, 128), 0) == (row & 127)).astype(F32).astype(BF))
        hist = dot(jnp.concatenate(high, 1), jnp.concatenate(low, 1), NT)[:8].astype(jnp.int32)
        for d in range(groups):
            out_ref[d, 8 * s : 8 * s + 8, :] = hist
    lines = left_ref.shape[1]
    rest = jnp.zeros((8 - 2 * buckets, 128), jnp.int32)
    counts = [count_ref[s] for s in range(buckets)]
    counts = jnp.concatenate(counts, 0)
    counts = jnp.concatenate([counts, jnp.zeros((buckets, 128 - counts.shape[1]), jnp.int32)], 1)
    for line in range(lines):
        pairs = [
            left_ref[s, line : line + 1, :] + (right_ref[s, line : line + 1, :] << 16)
            for s in range(buckets)
        ]
        block = jnp.concatenate(pairs + [counts, rest], 0)
        for d in range(line * groups // lines, (line + 1) * groups // lines):
            out_ref[d, hist_rows : hist_rows + 8, :] = block


def loop(n, step, carry):
    for i in range(n):
        carry = step(i, carry)
    return carry


def tie_kernel(held_ref, first_ref, out_ref):
    out_ref[...] = held_ref[...]


def one_hot(rows, at, shape):
    return ((iota(shape, 0) + at) == rows).astype(F32).astype(BF)


def spread_counts(hist, groups, mult_ref, a):
    hist = jnp.broadcast_to(hist[:, None, :], (groups, 8, 128)).reshape(128, 128)
    mult_ref[128 * a : 128 * (a + 1), :] = hist.T


def forward_kernel(buckets, which, neg_scale, me_ref, x_ref, *refs):
    first = which[0] == 0
    many = len(which)
    slab_refs, ops_hbm = refs[:many], refs[many]
    refs = refs[many + 1 :]
    if first:
        rel_acc, et0_ref = refs[:2]
        refs = refs[2:]
    else:
        et0_ref, sum_ref, rel_ref = refs[:3]
        refs = refs[3:]
    lrow_ref, qg_refs, pk_refs = refs[0], refs[1 : many + 1], refs[many + 1 : 2 * many + 1]
    refs = refs[2 * many + 1 :]
    oh_ref, whi_ref, wlo_ref, mult_ref, ops_ref, ops_sem = refs[:6]
    if not first:
        rel_acc, et_ref = refs[6:]
    ops_copy = pltpu.make_async_copy(ops_hbm, ops_ref, ops_sem)
    ops_copy.start()
    rel_own, width, _ = ops_hbm.shape
    groups = x_ref.shape[0]
    part_rows = slab_refs[0].shape[0]
    slots = rel_own * 128
    chunk = 256
    chunks = part_rows // chunk
    hist_rows = 8 * buckets
    me = me_ref[0]
    core = me & 1

    lane_row = iota((128, slots), 0)
    lane = iota((128, slots), 1)
    relation, slot = lane >> 7, lane & 7
    per_line = 128 // (8 * rel_own)
    pick_slot = (lane_row == (me % per_line) * (8 * rel_own) + relation * 8 + slot)
    pick_slot = pick_slot.astype(F32).astype(BF)
    pick_count = (lane_row == me * rel_own + relation).astype(F32).astype(BF)
    lane = iota((groups, slots), 1)
    own_group = iota((groups, slots), 0) == ((lane >> 3) & (groups - 1))
    slot_row = iota((1, slots), 1) & 7

    def own(values):
        return jnp.sum(jnp.where(own_group, values, 0.0), axis=0, keepdims=True)

    def narrow(values):
        return values.astype(F32).astype(BF)

    for at_call, s in enumerate(which):
        slab, pk = slab_refs[at_call], pk_refs[at_call]
        if not first:
            s = 1 + core if at_call == 0 else 2 - core
        pair = x_ref[:, hist_rows + s, :]
        left, right = pair & 65535, pair >> 16
        parts = [left >> 5, left & 31, right >> 5, right & 31]
        parts = dot(narrow(jnp.concatenate(parts, 0)), pick_slot)
        parts = [own(parts[groups * q : groups * (q + 1)]) for q in range(4)]
        left_row = (parts[0] * 32.0 + parts[1]).astype(jnp.int32)
        right_row = (parts[2] * 32.0 + parts[3]).astype(jnp.int32)
        count_row = own(dot(narrow(x_ref[:, hist_rows + buckets + s, :]), pick_count))
        live = (count_row.astype(jnp.int32) > slot_row).astype(F32)
        lrow_ref[at_call : at_call + 1, :] = left_row

        highs, lows = [], []
        for a in range(8):
            hist = x_ref[:, 8 * s + a, :]
            highs.append(hist >> 5)
            lows.append(hist & 31)
            spread_counts(hist.astype(F32), groups, mult_ref, a)
        for q, group in enumerate([highs[:4], highs[4:], lows[:4], lows[4:]]):
            at = width + 16 * q
            pk[at : at + 16, :] = narrow(jnp.concatenate(group, 1))

        slab_t = et0_ref if first else et_ref
        slab_t[...] = slab[...].T

        def left_hot(n, carry):
            at = n * chunk
            oh_ref[pl.ds(at, chunk), :] = one_hot(left_row, n * chunk, (chunk, slots))
            return carry

        def right_hot(n, carry):
            at = n * chunk
            oh_ref[pl.ds(at, chunk), :] = one_hot(right_row, n * chunk, (chunk, slots))
            return carry

        loop(chunks, left_hot, 0)
        left_t = dot(et0_ref[...], oh_ref[...]).astype(BF)
        if at_call == 0:
            ops_copy.wait()
        query_t = jnp.concatenate(
            [dot(ops_ref[i], left_t[:, 128 * i : 128 * (i + 1)], TN) for i in range(rel_own)], 1
        ).astype(BF)
        pk[0:width, :] = query_t
        half_t = query_t * 0.5
        loop(chunks, right_hot, 0)
        right_t = dot(slab_t[...], oh_ref[...])
        positive = jnp.sum(query_t.astype(F32) * right_t, axis=0, keepdims=True)
        pos_grad = -live * jax.nn.sigmoid(-positive)
        pos_high = pos_grad.astype(BF)
        pos_low = (pos_grad - pos_high.astype(F32)).astype(BF)
        misc = [narrow(parts[2]), narrow(parts[3]), narrow(live), pos_high, pos_low]
        misc = [row.astype(F32) for row in misc] + [jnp.zeros((11, slots), F32)]
        pk[width + 64 : width + 80, :] = jnp.concatenate(misc, 0).astype(BF)
        factor = live * (0.5 * neg_scale)

        def weigh(n, carry):
            at = n * chunk
            level = jnp.tanh(dot(slab[pl.ds(at, chunk), :], half_t))
            ngrad = (level * factor + factor).astype(BF).astype(F32)
            mult = mult_ref[pl.ds(at, chunk), :]
            weight = ngrad * jnp.concatenate([mult] * rel_own, 1)
            high = weight.astype(BF)
            whi_ref[pl.ds(at, chunk), :] = high
            wlo_ref[pl.ds(at, chunk), :] = (weight - high.astype(F32)).astype(BF)
            return carry

        loop(chunks, weigh, 0)
        qgrad_t = dot(slab_t[...], whi_ref[...]) + dot(slab_t[...], wlo_ref[...])
        qgrad_t = (qgrad_t + right_t * pos_grad).astype(BF)
        qg_refs[at_call][...] = qgrad_t
        for i in range(rel_own):
            cols = slice(128 * i, 128 * (i + 1))
            outer = dot(left_t[:, cols], qgrad_t[:, cols], NT)
            if first:
                rel_acc[i] = outer
            elif at_call == 0:
                rel_acc[i] = sum_ref[i] + outer
            else:
                rel_acc[i] = rel_acc[i] + outer

    if first:
        return
    doms, held, _ = rel_ref.shape
    held = held // rel_own
    for d in range(doms):
        block = [rel_acc[i, held * d : held * (d + 1), :] for i in range(rel_own)]
        rel_ref[d] = jnp.concatenate(block, 0).astype(BF)


def entity_kernel(buckets, neg_scale, groups, me_ref, slab_ref, ops_hbm, *refs):
    lrow0_ref, lrow_ref = refs[:2]
    qg_refs, pk_refs = refs[2 : 2 + buckets], refs[2 + buckets : 2 + 2 * buckets]
    keep_ref, send_ref, rows_ref, mult_ref, ops_ref, ops_sem = refs[2 + 2 * buckets :]
    ops_copy = pltpu.make_async_copy(ops_hbm, ops_ref, ops_sem)
    ops_copy.start()
    me = me_ref[0]
    rel_own, width, _ = ops_hbm.shape
    part_rows = slab_ref.shape[0]
    slots = rel_own * 128
    chunk = 256
    chunks = part_rows // chunk
    share = part_rows // groups
    for s in range(buckets):
        pk = pk_refs[s]
        left_row = lrow_ref[s - 1 : s, :] if s else lrow0_ref[0:1, :]
        if s == 0:
            ops_copy.wait()
        qgrad_t = qg_refs[s][...]
        lgrad_t = jnp.concatenate(
            [dot(ops_ref[i], qgrad_t[:, 128 * i : 128 * (i + 1)]) for i in range(rel_own)], 1
        ).astype(BF)
        hist = pk[width : width + 64, :].astype(F32)
        hist = hist[:32] * 32.0 + hist[32:]
        for a in range(8):
            cols = slice(128 * (a % 4), 128 * (a % 4 + 1))
            spread_counts(hist[16 * (a // 4) : 16 * (a // 4 + 1), cols], groups, mult_ref, a)
        misc = pk[width + 64 : width + 80, :].astype(F32)
        right_row = (misc[0:1] * 32.0 + misc[1:2]).astype(jnp.int32)
        factor = misc[2:3] * (0.5 * neg_scale)
        pos_grad = misc[3:4] + misc[4:5]
        query_t = pk[0:width, :]
        half_t = query_t * 0.5

        def weigh(n, carry):
            at = n * chunk
            level = jnp.tanh(dot(slab_ref[pl.ds(at, chunk), :], half_t))
            ngrad = (level * factor + factor).astype(BF).astype(F32)
            mult = mult_ref[pl.ds(at, chunk), :]
            hit = (iota((chunk, slots), 0) + n * chunk) == right_row
            weight = ngrad * jnp.concatenate([mult] * rel_own, 1) + jnp.where(hit, pos_grad, 0.0)
            high = weight.astype(BF)
            low = (weight - high.astype(F32)).astype(BF)
            hot = one_hot(left_row, n * chunk, (chunk, slots))
            rows = dot(high, query_t, NT) + dot(low, query_t, NT) + dot(hot, lgrad_t, NT)
            rows_ref[pl.ds(at, chunk), :] = rows if s == 0 else rows_ref[pl.ds(at, chunk), :] + rows
            return carry

        loop(chunks, weigh, 0)
    for n in range(groups):
        to = me ^ (((n >> 1) & 3) * 4 + (n & 1) * 2 + (n >> 3))
        block = rows_ref[pl.ds(pl.multiple_of(to * share, share), share), :]
        half = groups // 2
        if n < half:
            keep_ref[n] = block
        else:
            send_ref[n - half] = block


def shards(entities, operators, left_rows, right_rows, negatives, counts):
    buckets = left_rows.shape[0]
    slot_count = left_rows.shape[-1]
    neg_count = negatives.shape[-1]
    groups = lax.axis_size("span")
    doms = lax.axis_size("dom")
    rel_own = operators.shape[0]
    relations = rel_own * groups
    part_rows, width = entities.shape
    neg_scale = float(neg_count) ** (-0.5)
    share = part_rows // groups
    slots = rel_own * 128
    limit = pltpu.CompilerParams(vmem_limit_bytes=12 * 1024 * 1024)
    small = pltpu.CompilerParams(vmem_limit_bytes=2 * 1024 * 1024)

    packed = pl.pallas_call(
        functools.partial(pack_kernel, buckets, groups),
        out_shape=jax.ShapeDtypeStruct((groups, 8 * buckets + 8, 128), jnp.int32),
        in_specs=[VMEM] * 4,
        out_specs=VMEM,
        name="pack_lists",
    )(
        negatives.reshape(buckets, neg_count // 128, 128),
        left_rows.reshape(buckets, slot_count // 128, 128),
        right_rows.reshape(buckets, slot_count // 128, 128),
        counts.reshape(buckets, 1, relations),
    )
    received = exchanged(packed, "span")
    near = shifted(entities, -1, -2)
    near = pl.pallas_call(
        tie_kernel,
        out_shape=jax.ShapeDtypeStruct(entities.shape, BF),
        in_specs=[VMEM, VMEM],
        out_specs=VMEM,
        compiler_params=small,
        name="after_lists",
    )(near, received)
    slabs = [near, swapped(near, 1)]

    me = lax.axis_index("span").astype(jnp.int32).reshape(1)
    wide = pltpu.VMEM((part_rows, slots), BF)

    def scratch_of():
        return [
            wide,
            wide,
            wide,
            pltpu.VMEM((part_rows, 128), F32),
            pltpu.VMEM(operators.shape, BF),
            pltpu.SemaphoreType.DMA,
        ]

    def packs_of(many):
        return (
            [jax.ShapeDtypeStruct((8, slots), jnp.int32)]
            + [jax.ShapeDtypeStruct((width, slots), BF)] * many
            + [jax.ShapeDtypeStruct((width + 80, slots), BF)] * many
        )

    rel_sum, slab_t, lrow_own, qg_own, pack_own = pl.pallas_call(
        functools.partial(forward_kernel, buckets, (0,), neg_scale),
        out_shape=[
            jax.ShapeDtypeStruct((rel_own, width, width), F32),
            jax.ShapeDtypeStruct((width, part_rows), BF),
        ]
        + packs_of(1),
        in_specs=[SMEM, VMEM, VMEM, HBM],
        out_specs=[VMEM] * 5,
        scratch_shapes=scratch_of(),
        compiler_params=limit,
        cost_estimate=pl.CostEstimate(
            flops=1_400_000_000, bytes_accessed=2_000_000, transcendentals=500_000
        ),
        name="own_bucket",
    )(me, received, entities, operators)
    others = tuple(range(1, buckets))
    rel_parts, lrow_other, *packs = pl.pallas_call(
        functools.partial(forward_kernel, buckets, others, neg_scale),
        out_shape=[jax.ShapeDtypeStruct((doms, rel_own * width // doms, width), BF)]
        + packs_of(buckets - 1),
        in_specs=[SMEM] + [VMEM] * buckets + [HBM, VMEM, VMEM],
        out_specs=[VMEM] * (2 * buckets),
        scratch_shapes=scratch_of()
        + [pltpu.VMEM((rel_own, width, width), F32), pltpu.VMEM((width, part_rows), BF)],
        compiler_params=limit,
        cost_estimate=pl.CostEstimate(
            flops=3_000_000_000, bytes_accessed=3_000_000, transcendentals=1_100_000
        ),
        name="other_buckets",
    )(me, received, *slabs, operators, slab_t, rel_sum)
    grads = [qg_own] + packs[:2]
    packs = [pack_own, shifted(packs[2], 1, 2), shifted(packs[3], 2, 1)]
    rel_arrived = exchanged(rel_parts, "dom")

    half_parts = jax.ShapeDtypeStruct((groups // 2, share, width), F32)
    keep, send = pl.pallas_call(
        functools.partial(entity_kernel, buckets, neg_scale, groups),
        out_shape=(half_parts, half_parts),
        in_specs=[SMEM, VMEM, HBM] + [VMEM] * (2 + 2 * buckets),
        out_specs=(VMEM, VMEM),
        scratch_shapes=[
            pltpu.VMEM((part_rows, width), F32),
            pltpu.VMEM((part_rows, 128), F32),
            pltpu.VMEM(operators.shape, BF),
            pltpu.SemaphoreType.DMA,
        ],
        compiler_params=limit,
        cost_estimate=pl.CostEstimate(
            flops=4_000_000_000, bytes_accessed=3_000_000, transcendentals=1_600_000
        ),
        name="entity_gradients",
    )(me, entities, operators, lrow_own, lrow_other, *grads, *packs)

    total = keep + swapped(send, 1)
    total = total.reshape(4, 2, share, width)
    got = [swapped(total[x].astype(BF), 4 * x) for x in (1, 2, 3)]
    total = total[0] + sum(part.astype(F32) for part in got)
    entity_share = total[0] + swapped(total[1], 2)
    rel_share = jnp.sum(rel_arrived.astype(F32), axis=0)
    return (entity_share, rel_share.reshape(rel_own, width // doms, width))


def solution(mesh):
    in_specs = (
        P("dom", None),
        P("span", None, None),
        P(None, "dom", "span", None),
        P(None, "dom", "span", None),
        P(None, "dom", "span", None),
        P(None, "dom", "span", None),
    )
    out_specs = (P(("dom", "span"), None), P("span", "dom", None))
    return jax.shard_map(shards, mesh=mesh, in_specs=in_specs, out_specs=out_specs, check_vma=False)
```

```python
import functools

import jax
import jax.numpy as jnp
from jax import lax
from jax.experimental import pallas as pl
from jax.experimental.pallas import tpu as pltpu
from jax.sharding import PartitionSpec as P

BF = jnp.bfloat16
F32 = jnp.float32
NT = (((1,), (1,)), ((), ()))
TN = (((0,), (0,)), ((), ()))
VMEM = pl.BlockSpec(memory_space=pltpu.VMEM)
SMEM = pl.BlockSpec(memory_space=pltpu.SMEM)
HBM = pl.BlockSpec(memory_space=pltpu.HBM)


def dot(a, b, dims=(((1,), (0,)), ((), ()))):
    return lax.dot_general(a, b, dims, preferred_element_type=F32)


def shifted(value, step, other):
    doms, groups = lax.axis_size("dom"), lax.axis_size("span")
    pairs = []
    for p in range(doms):
        for c in range(groups):
            to = (p + (other if c & 1 else step)) % doms
            pairs.append((p * groups + c, to * groups + c))
    return lax.ppermute(value, ("dom", "span"), pairs)


def swapped(value, bits):
    groups = lax.axis_size("span")
    return lax.ppermute(value, "span", [(i, i ^ bits) for i in range(groups)])


def exchanged(value, axis):
    return lax.all_to_all(value, axis, split_axis=0, concat_axis=0, tiled=True)


def iota(shape, axis):
    return lax.broadcasted_iota(jnp.int32, shape, axis)


def pack_kernel(
    groups, neg_ref, left_ref, right_ref, count_ref, ent_ref, out_ref, slab_ref, sem
):
    slab_copy = pltpu.make_async_copy(ent_ref, slab_ref, sem)
    slab_copy.start()
    hists = []
    for s in range(3):
        high, low = [], []
        for q in range(neg_ref.shape[1]):
            row = neg_ref[s, q : q + 1, :]
            high.append((iota((16, 128), 0) == (row >> 7)).astype(F32).astype(BF))
            low.append((iota((128, 128), 0) == (row & 127)).astype(F32).astype(BF))
        hist = dot(jnp.concatenate(high, 1), jnp.concatenate(low, 1), NT)[:8]
        hists.append(hist.astype(jnp.int32))
    words = hists[0] + (hists[1] << 16)
    for d in range(groups):
        out_ref[d, 0:8, :] = words
    lines = left_ref.shape[1]
    counts = [count_ref[s] for s in range(3)]
    counts = counts + [jnp.zeros(counts[0].shape, jnp.int32)]
    counts = [jnp.concatenate(counts[:2], 1), jnp.concatenate(counts[2:], 1)]
    for line in range(lines):
        rows = [ref[s, line : line + 1, :] for ref in (left_ref, right_ref) for s in range(3)]
        words = hists[2] + (jnp.concatenate(rows + counts, 0) << 16)
        for d in range(line * groups // lines, (line + 1) * groups // lines):
            out_ref[d, 8:16, :] = words
    slab_copy.wait()


def loop(n, step, carry):
    for i in range(n):
        carry = step(i, carry)
    return carry


def tie_kernel(held_ref, first_ref, out_ref):
    out_ref[...] = held_ref[...]


def one_hot(rows, at, shape):
    return ((iota(shape, 0) + at) == rows).astype(F32).astype(BF)


def spread_counts(hist, groups, mult_ref, a):
    hist = jnp.broadcast_to(hist[:, None, :], (groups, 8, 128)).reshape(128, 128)
    mult_ref[128 * a : 128 * (a + 1), :] = hist.T


def forward_kernel(buckets, which, neg_scale, me_ref, x_ref, *refs):
    first = which[0] == 0
    many = len(which)
    slab_refs, ops_hbm = refs[:many], refs[many]
    refs = refs[many + 1 :]
    if first:
        rel_acc, et0_ref = refs[:2]
        refs = refs[2:]
    else:
        et0_ref, sum_ref, rel_ref = refs[:3]
        refs = refs[3:]
    lrow_ref, qg_hbms, pk_refs = refs[0], refs[1 : many + 1], refs[many + 1 : 2 * many + 1]
    refs = refs[2 * many + 1 :]
    oh_ref, whi_ref, wlo_ref, mult_ref, ops_ref, qg_ref, ops_sem, qg_sems = refs[:8]
    qg_copies = [
        pltpu.make_async_copy(qg_ref.at[n], qg_hbms[n], qg_sems.at[n]) for n in range(many)
    ]
    if first:
        pk_hbm, pk_refs = pk_refs[0], refs[8:9]
        pk_copy = pltpu.make_async_copy(pk_refs[0], pk_hbm, refs[9])
    else:
        rel_acc, et_ref = refs[8:]
    ops_copy = pltpu.make_async_copy(ops_hbm, ops_ref, ops_sem)
    ops_copy.start()
    rel_own, width, _ = ops_hbm.shape
    groups = x_ref.shape[0]
    part_rows = slab_refs[0].shape[0]
    slots = rel_own * 128
    chunk = 256
    chunks = part_rows // chunk
    me = me_ref[0]
    core = me & 1

    lane_row = iota((128, slots), 0)
    lane = iota((128, slots), 1)
    relation, slot = lane >> 7, lane & 7
    per_line = 128 // (8 * rel_own)
    pick_slot = (lane_row == (me % per_line) * (8 * rel_own) + relation * 8 + slot)
    pick_slot = pick_slot.astype(F32).astype(BF)
    count_lane = me * rel_own + relation
    lane = iota((groups, slots), 1)
    own_group = iota((groups, slots), 0) == ((lane >> 3) & (groups - 1))
    slot_row = iota((1, slots), 1) & 7

    def own(values):
        return jnp.sum(jnp.where(own_group, values, 0.0), axis=0, keepdims=True)

    def narrow(values):
        return values.astype(F32).astype(BF)

    for at_call, s in enumerate(which):
        slab, pk = slab_refs[at_call], pk_refs[at_call]
        if not first:
            s = 1 + core if at_call == 0 else 2 - core
        left, right = x_ref[:, 8 + s, :] >> 16, x_ref[:, 11 + s, :] >> 16
        parts = [left >> 5, left & 31, right >> 5, right & 31]
        parts = dot(narrow(jnp.concatenate(parts, 0)), pick_slot)
        parts = [own(parts[groups * q : groups * (q + 1)]) for q in range(4)]
        left_row = (parts[0] * 32.0 + parts[1]).astype(jnp.int32)
        right_row = (parts[2] * 32.0 + parts[3]).astype(jnp.int32)
        pick_count = narrow(lane_row == count_lane + (s % 2) * (groups * rel_own))
        count_row = own(dot(narrow(x_ref[:, 14 + s // 2, :] >> 16), pick_count))
        live = (count_row.astype(jnp.int32) > slot_row).astype(F32)
        lrow_ref[at_call : at_call + 1, :] = left_row

        highs, lows = [], []
        for a in range(8):
            hist = (x_ref[:, (s // 2) * 8 + a, :] >> (16 * (s % 2))) & 65535
            highs.append(hist >> 5)
            lows.append(hist & 31)
            spread_counts(hist.astype(F32), groups, mult_ref, a)
        for q, group in enumerate([highs[:4], highs[4:], lows[:4], lows[4:]]):
            at = width + 16 * q
            pk[at : at + 16, :] = narrow(jnp.concatenate(group, 1))

        slab_t = et0_ref if first else et_ref
        slab_t[...] = slab[...].T

        def left_hot(n, carry):
            at = n * chunk
            oh_ref[pl.ds(at, chunk), :] = one_hot(left_row, n * chunk, (chunk, slots))
            return carry

        def right_hot(n, carry):
            at = n * chunk
            oh_ref[pl.ds(at, chunk), :] = one_hot(right_row, n * chunk, (chunk, slots))
            return carry

        loop(chunks, left_hot, 0)
        left_t = dot(et0_ref[...], oh_ref[...]).astype(BF)
        if at_call == 0:
            ops_copy.wait()
        query_t = jnp.concatenate(
            [dot(ops_ref[i], left_t[:, 128 * i : 128 * (i + 1)], TN) for i in range(rel_own)], 1
        ).astype(BF)
        pk[0:width, :] = query_t
        half_t = query_t * 0.5
        loop(chunks, right_hot, 0)
        right_t = dot(slab_t[...], oh_ref[...])
        positive = jnp.sum(query_t.astype(F32) * right_t, axis=0, keepdims=True)
        pos_grad = -live * jax.nn.sigmoid(-positive)
        pos_high = pos_grad.astype(BF)
        pos_low = (pos_grad - pos_high.astype(F32)).astype(BF)
        misc = [narrow(parts[2]), narrow(parts[3]), narrow(live), pos_high, pos_low]
        misc = [row.astype(F32) for row in misc] + [jnp.zeros((11, slots), F32)]
        pk[width + 64 : width + 80, :] = jnp.concatenate(misc, 0).astype(BF)
        if first:
            pk_copy.start()
        factor = live * (0.5 * neg_scale)

        def weigh(n, carry):
            at = n * chunk
            level = jnp.tanh(dot(slab[pl.ds(at, chunk), :], half_t))
            ngrad = (level * factor + factor).astype(BF).astype(F32)
            mult = mult_ref[pl.ds(at, chunk), :]
            weight = ngrad * jnp.concatenate([mult] * rel_own, 1)
            high = weight.astype(BF)
            whi_ref[pl.ds(at, chunk), :] = high
            wlo_ref[pl.ds(at, chunk), :] = (weight - high.astype(F32)).astype(BF)
            return carry

        loop(chunks, weigh, 0)
        qgrad_t = dot(slab_t[...], whi_ref[...]) + dot(slab_t[...], wlo_ref[...])
        qgrad_t = (qgrad_t + right_t * pos_grad).astype(BF)
        qg_ref[at_call] = qgrad_t
        qg_copies[at_call].start()
        for i in range(rel_own):
            cols = slice(128 * i, 128 * (i + 1))
            outer = dot(left_t[:, cols], qgrad_t[:, cols], NT)
            if first:
                rel_acc[i] = outer
            elif at_call == 0:
                rel_acc[i] = sum_ref[i] + outer
            else:
                rel_acc[i] = rel_acc[i] + outer

    if first:
        pk_copy.wait()
        qg_copies[0].wait()
        return
    doms, held, _ = rel_ref.shape
    held = held // rel_own
    for d in range(doms):
        block = [rel_acc[i, held * d : held * (d + 1), :] for i in range(rel_own)]
        rel_ref[d] = jnp.concatenate(block, 0).astype(BF)
    for copy in qg_copies:
        copy.wait()


def entity_kernel(buckets, neg_scale, groups, me_ref, slab_ref, ops_hbm, *refs):
    lrow0_ref, lrow_ref = refs[:2]
    qg_hbms, pk_refs = refs[2 : 2 + buckets], list(refs[2 + buckets : 2 + 2 * buckets])
    keep_ref, send_ref, rows_ref, mult_ref, ops_ref, qg_ref, pk_ref, sems = refs[2 + 2 * buckets :]
    copies = [
        pltpu.make_async_copy(ops_hbm, ops_ref, sems.at[0]),
        pltpu.make_async_copy(pk_refs[0], pk_ref, sems.at[1]),
    ]
    for s in range(buckets):
        copies.append(pltpu.make_async_copy(qg_hbms[s], qg_ref.at[s], sems.at[2 + s]))
    for copy in copies:
        copy.start()
    pk_refs[0] = pk_ref
    me = me_ref[0]
    rel_own, width, _ = ops_hbm.shape
    part_rows = slab_ref.shape[0]
    slots = rel_own * 128
    chunk = 256
    chunks = part_rows // chunk
    share = part_rows // groups
    for step, s in enumerate(list(range(1, buckets)) + [0]):
        pk = pk_refs[s]
        left_row = lrow_ref[s - 1 : s, :] if s else lrow0_ref[0:1, :]
        hist = pk[width : width + 64, :].astype(F32)
        hist = hist[:32] * 32.0 + hist[32:]
        for a in range(8):
            cols = slice(128 * (a % 4), 128 * (a % 4 + 1))
            spread_counts(hist[16 * (a // 4) : 16 * (a // 4 + 1), cols], groups, mult_ref, a)
        misc = pk[width + 64 : width + 80, :].astype(F32)
        right_row = (misc[0:1] * 32.0 + misc[1:2]).astype(jnp.int32)
        factor = misc[2:3] * (0.5 * neg_scale)
        pos_grad = misc[3:4] + misc[4:5]
        query_t = pk[0:width, :]
        half_t = query_t * 0.5
        if step == 0:
            for copy in copies:
                copy.wait()
        qgrad_t = qg_ref[s]
        lgrad_t = jnp.concatenate(
            [dot(ops_ref[i], qgrad_t[:, 128 * i : 128 * (i + 1)]) for i in range(rel_own)], 1
        ).astype(BF)

        def weigh(n, carry):
            at = n * chunk
            level = jnp.tanh(dot(slab_ref[pl.ds(at, chunk), :], half_t))
            ngrad = (level * factor + factor).astype(BF).astype(F32)
            mult = mult_ref[pl.ds(at, chunk), :]
            hit = (iota((chunk, slots), 0) + n * chunk) == right_row
            weight = ngrad * jnp.concatenate([mult] * rel_own, 1) + jnp.where(hit, pos_grad, 0.0)
            high = weight.astype(BF)
            low = (weight - high.astype(F32)).astype(BF)
            hot = one_hot(left_row, n * chunk, (chunk, slots))
            rows = dot(high, query_t, NT) + dot(low, query_t, NT) + dot(hot, lgrad_t, NT)
            rows_ref[pl.ds(at, chunk), :] = rows if step == 0 else rows_ref[pl.ds(at, chunk), :] + rows
            return carry

        loop(chunks, weigh, 0)
    for n in range(groups):
        to = me ^ (((n >> 1) & 3) * 4 + (n & 1) * 2 + (n >> 3))
        block = rows_ref[pl.ds(pl.multiple_of(to * share, share), share), :]
        half = groups // 2
        if n < half:
            keep_ref[n] = block
        else:
            send_ref[n - half] = block


def finish_kernel(keep_ref, got_ref, parts_hbm, ent_ref, rel_ref, parts_ref, sems):
    cuts = parts_ref.shape[0]
    copies = [pltpu.make_async_copy(parts_hbm.at[n], parts_ref.at[n], sems.at[n]) for n in range(cuts)]
    for copy in copies:
        copy.start()
    ent_ref[...] = keep_ref[...] + got_ref[...]
    total = None
    for n in range(cuts):
        copies[n].wait()
        part = jnp.sum(parts_ref[n].astype(F32), axis=0)
        total = part if total is None else total + part
    rel_ref[...] = total


def shards(entities, operators, left_rows, right_rows, negatives, counts):
    buckets = left_rows.shape[0]
    slot_count = left_rows.shape[-1]
    neg_count = negatives.shape[-1]
    groups = lax.axis_size("span")
    doms = lax.axis_size("dom")
    rel_own = operators.shape[0]
    relations = rel_own * groups
    part_rows, width = entities.shape
    neg_scale = float(neg_count) ** (-0.5)
    share = part_rows // groups
    slots = rel_own * 128
    limit = pltpu.CompilerParams(vmem_limit_bytes=12 * 1024 * 1024)
    small = pltpu.CompilerParams(vmem_limit_bytes=2 * 1024 * 1024)

    packed, slab = pl.pallas_call(
        functools.partial(pack_kernel, groups),
        out_shape=(
            jax.ShapeDtypeStruct((groups, 16, 128), jnp.int32),
            jax.ShapeDtypeStruct(entities.shape, BF),
        ),
        in_specs=[VMEM] * 4 + [HBM],
        out_specs=(VMEM, VMEM),
        scratch_shapes=[pltpu.SemaphoreType.DMA],
        name="pack_lists",
    )(
        negatives.reshape(buckets, neg_count // 128, 128),
        left_rows.reshape(buckets, slot_count // 128, 128),
        right_rows.reshape(buckets, slot_count // 128, 128),
        counts.reshape(buckets, 1, relations),
        entities,
    )
    received = exchanged(packed, "span")
    near = shifted(slab, -1, -2)
    near = pl.pallas_call(
        tie_kernel,
        out_shape=jax.ShapeDtypeStruct(entities.shape, BF),
        in_specs=[VMEM, VMEM],
        out_specs=VMEM,
        compiler_params=small,
        name="after_lists",
    )(near, received)
    slabs = [near, swapped(near, 1)]

    me = lax.axis_index("span").astype(jnp.int32).reshape(1)
    wide = pltpu.VMEM((part_rows, slots), BF)

    def scratch_of(many):
        return [
            wide,
            wide,
            wide,
            pltpu.VMEM((part_rows, 128), F32),
            pltpu.VMEM(operators.shape, BF),
            pltpu.VMEM((many, width, slots), BF),
            pltpu.SemaphoreType.DMA,
            pltpu.SemaphoreType.DMA((many,)),
        ]

    def packs_of(many, pack):
        return (
            [jax.ShapeDtypeStruct((8, slots), jnp.int32)]
            + [pltpu.HBM((width, slots), BF)] * many
            + [pack((width + 80, slots), BF)] * many
        )

    rel_sum, slab_t, lrow_own, qg_own, pack_own = pl.pallas_call(
        functools.partial(forward_kernel, buckets, (0,), neg_scale),
        out_shape=[
            jax.ShapeDtypeStruct((rel_own, width, width), F32),
            jax.ShapeDtypeStruct((width, part_rows), BF),
        ]
        + packs_of(1, pltpu.HBM),
        in_specs=[SMEM, VMEM, VMEM, HBM],
        out_specs=[VMEM] * 3 + [HBM] * 2,
        scratch_shapes=scratch_of(1)
        + [pltpu.VMEM((width + 80, slots), BF), pltpu.SemaphoreType.DMA],
        compiler_params=limit,
        cost_estimate=pl.CostEstimate(
            flops=1_400_000_000, bytes_accessed=2_000_000, transcendentals=500_000
        ),
        name="own_bucket",
    )(me, received, slab, operators)
    others = tuple(range(1, buckets))
    rel_parts, lrow_other, *packs = pl.pallas_call(
        functools.partial(forward_kernel, buckets, others, neg_scale),
        out_shape=[jax.ShapeDtypeStruct((doms, rel_own * width // doms, width), BF)]
        + packs_of(buckets - 1, jax.ShapeDtypeStruct),
        in_specs=[SMEM] + [VMEM] * buckets + [HBM, VMEM, VMEM],
        out_specs=[VMEM] * 2 + [HBM] * (buckets - 1) + [VMEM] * (buckets - 1),
        scratch_shapes=scratch_of(buckets - 1)
        + [pltpu.VMEM((rel_own, width, width), F32), pltpu.VMEM((width, part_rows), BF)],
        compiler_params=limit,
        cost_estimate=pl.CostEstimate(
            flops=3_000_000_000, bytes_accessed=3_000_000, transcendentals=1_100_000
        ),
        name="other_buckets",
    )(me, received, *slabs, operators, slab_t, rel_sum)
    pack_own = pltpu.with_memory_space_constraint(pack_own, pltpu.HBM)
    grads = [pltpu.with_memory_space_constraint(grad, pltpu.HBM) for grad in [qg_own] + packs[:2]]
    packs = [pack_own, shifted(packs[2], 1, 2), shifted(packs[3], 2, 1)]
    rel_arrived = exchanged(rel_parts, "dom")

    half_parts = jax.ShapeDtypeStruct((groups // 2, share, width), F32)
    keep, send = pl.pallas_call(
        functools.partial(entity_kernel, buckets, neg_scale, groups),
        out_shape=(half_parts, half_parts),
        in_specs=[SMEM, VMEM, HBM, VMEM, VMEM] + [HBM] * (buckets + 1) + [VMEM] * (buckets - 1),
        out_specs=(VMEM, VMEM),
        scratch_shapes=[
            pltpu.VMEM((part_rows, width), F32),
            pltpu.VMEM((part_rows, 128), F32),
            pltpu.VMEM(operators.shape, BF),
            pltpu.VMEM((buckets, width, slots), BF),
            pltpu.VMEM((width + 80, slots), BF),
            pltpu.SemaphoreType.DMA((buckets + 2,)),
        ],
        compiler_params=limit,
        cost_estimate=pl.CostEstimate(
            flops=4_000_000_000, bytes_accessed=3_000_000, transcendentals=1_600_000
        ),
        name="entity_gradients",
    )(me, slab, operators, lrow_own, lrow_other, *grads, *packs)

    total = keep + swapped(send, 1)
    total = total.reshape(4, 2, share, width)
    got = [swapped(total[x].astype(BF), 4 * x) for x in (1, 2, 3)]
    total = total[0] + sum(part.astype(F32) for part in got)
    held = rel_own * width // doms
    rel_arrived = rel_arrived.reshape(4, doms // 4, held, width)
    entity_share, rel_share = pl.pallas_call(
        finish_kernel,
        out_shape=(
            jax.ShapeDtypeStruct((share, width), F32),
            jax.ShapeDtypeStruct((held, width), F32),
        ),
        in_specs=[VMEM, VMEM, HBM],
        out_specs=(VMEM, VMEM),
        scratch_shapes=[
            pltpu.VMEM(rel_arrived.shape, BF),
            pltpu.SemaphoreType.DMA((4,)),
        ],
        compiler_params=small,
        name="last_sums",
    )(total[0], swapped(total[1], 2), rel_arrived)
    return (entity_share, rel_share.reshape(rel_own, width // doms, width))


def solution(mesh):
    in_specs = (
        P("dom", None),
        P("span", None, None),
        P(None, "dom", "span", None),
        P(None, "dom", "span", None),
        P(None, "dom", "span", None),
        P(None, "dom", "span", None),
    )
    out_specs = (P(("dom", "span"), None), P("span", "dom", None))
    return jax.shard_map(shards, mesh=mesh, in_specs=in_specs, out_specs=out_specs, check_vma=False)
```

```python
import functools

import jax
import jax.numpy as jnp
from jax import lax
from jax.experimental import pallas as pl
from jax.experimental.pallas import tpu as pltpu
from jax.sharding import PartitionSpec as P

BF = jnp.bfloat16
F32 = jnp.float32
NT = (((1,), (1,)), ((), ()))
TN = (((0,), (0,)), ((), ()))
VMEM = pl.BlockSpec(memory_space=pltpu.VMEM)
SMEM = pl.BlockSpec(memory_space=pltpu.SMEM)
HBM = pl.BlockSpec(memory_space=pltpu.HBM)


def dot(a, b, dims=(((1,), (0,)), ((), ()))):
    return lax.dot_general(a, b, dims, preferred_element_type=F32)


def shifted(value, step, other):
    doms, groups = lax.axis_size("dom"), lax.axis_size("span")
    pairs = []
    for p in range(doms):
        for c in range(groups):
            to = (p + (other if c & 1 else step)) % doms
            pairs.append((p * groups + c, to * groups + c))
    return lax.ppermute(value, ("dom", "span"), pairs)


def swapped(value, bits):
    groups = lax.axis_size("span")
    return lax.ppermute(value, "span", [(i, i ^ bits) for i in range(groups)])


def exchanged(value, axis):
    return lax.all_to_all(value, axis, split_axis=0, concat_axis=0, tiled=True)


def iota(shape, axis):
    return lax.broadcasted_iota(jnp.int32, shape, axis)


def pack_kernel(groups, neg_ref, left_ref, right_ref, count_ref, out_ref):
    hists = []
    for s in range(3):
        high, low = [], []
        for q in range(neg_ref.shape[1]):
            row = neg_ref[s, q : q + 1, :]
            high.append((iota((16, 128), 0) == (row >> 7)).astype(F32).astype(BF))
            low.append((iota((128, 128), 0) == (row & 127)).astype(F32).astype(BF))
        hist = dot(jnp.concatenate(high, 1), jnp.concatenate(low, 1), NT)[:8]
        hists.append(hist.astype(jnp.int32))
    words = hists[0] + (hists[1] << 16)
    for d in range(groups):
        out_ref[d, 0:8, :] = words
    lines = left_ref.shape[1]
    counts = [count_ref[s] for s in range(3)]
    counts = counts + [jnp.zeros(counts[0].shape, jnp.int32)]
    counts = [jnp.concatenate(counts[:2], 1), jnp.concatenate(counts[2:], 1)]
    for line in range(lines):
        rows = [ref[s, line : line + 1, :] for ref in (left_ref, right_ref) for s in range(3)]
        words = hists[2] + (jnp.concatenate(rows + counts, 0) << 16)
        for d in range(line * groups // lines, (line + 1) * groups // lines):
            out_ref[d, 8:16, :] = words


def loop(n, step, carry):
    for i in range(n):
        carry = step(i, carry)
    return carry


def tie_kernel(held_ref, first_ref, out_ref):
    out_ref[...] = held_ref[...]


def one_hot(rows, at, shape):
    return ((iota(shape, 0) + at) == rows).astype(F32).astype(BF)


def spread_counts(hist, groups, mult_ref, a):
    hist = jnp.broadcast_to(hist[:, None, :], (groups, 8, 128)).reshape(128, 128)
    mult_ref[128 * a : 128 * (a + 1), :] = hist.T


def forward_kernel(buckets, which, neg_scale, me_ref, x_ref, *refs):
    first = which[0] == 0
    many = len(which)
    slab_refs, ops_hbm = refs[:many], refs[many]
    refs = refs[many + 1 :]
    if first:
        rel_acc, et0_ref = refs[:2]
        refs = refs[2:]
    else:
        et0_ref, sum_ref, rel_ref = refs[:3]
        refs = refs[3:]
    lrow_ref, qg_hbms, pk_refs = refs[0], refs[1 : many + 1], refs[many + 1 : 2 * many + 1]
    refs = refs[2 * many + 1 :]
    oh_ref, whi_ref, wlo_ref, mult_ref, ops_ref, qg_ref, ops_sem, qg_sems = refs[:8]
    qg_copies = [
        pltpu.make_async_copy(qg_ref.at[n], qg_hbms[n], qg_sems.at[n]) for n in range(many)
    ]
    if first:
        pk_hbm, pk_refs = pk_refs[0], refs[8:9]
        pk_copy = pltpu.make_async_copy(pk_refs[0], pk_hbm, refs[9])
    else:
        rel_acc, et_ref = refs[8:]
    ops_copy = pltpu.make_async_copy(ops_hbm, ops_ref, ops_sem)
    ops_copy.start()
    rel_own, width, _ = ops_hbm.shape
    groups = x_ref.shape[0]
    part_rows = slab_refs[0].shape[0]
    slots = rel_own * 128
    chunk = 256
    chunks = part_rows // chunk
    me = me_ref[0]
    core = me & 1

    lane_row = iota((128, slots), 0)
    lane = iota((128, slots), 1)
    relation, slot = lane >> 7, lane & 7
    per_line = 128 // (8 * rel_own)
    pick_slot = (lane_row == (me % per_line) * (8 * rel_own) + relation * 8 + slot)
    pick_slot = pick_slot.astype(F32).astype(BF)
    count_lane = me * rel_own + relation
    lane = iota((groups, slots), 1)
    own_group = iota((groups, slots), 0) == ((lane >> 3) & (groups - 1))
    slot_row = iota((1, slots), 1) & 7

    def own(values):
        return jnp.sum(jnp.where(own_group, values, 0.0), axis=0, keepdims=True)

    def narrow(values):
        return values.astype(F32).astype(BF)

    for at_call, s in enumerate(which):
        slab, pk = slab_refs[at_call], pk_refs[at_call]
        if not first:
            s = 1 + core if at_call == 0 else 2 - core
        left, right = x_ref[:, 8 + s, :] >> 16, x_ref[:, 11 + s, :] >> 16
        parts = [left >> 5, left & 31, right >> 5, right & 31]
        parts = dot(narrow(jnp.concatenate(parts, 0)), pick_slot)
        parts = [own(parts[groups * q : groups * (q + 1)]) for q in range(4)]
        left_row = (parts[0] * 32.0 + parts[1]).astype(jnp.int32)
        right_row = (parts[2] * 32.0 + parts[3]).astype(jnp.int32)
        pick_count = narrow(lane_row == count_lane + (s % 2) * (groups * rel_own))
        count_row = own(dot(narrow(x_ref[:, 14 + s // 2, :] >> 16), pick_count))
        live = (count_row.astype(jnp.int32) > slot_row).astype(F32)
        lrow_ref[at_call : at_call + 1, :] = left_row

        highs, lows = [], []
        for a in range(8):
            hist = (x_ref[:, (s // 2) * 8 + a, :] >> (16 * (s % 2))) & 65535
            highs.append(hist >> 5)
            lows.append(hist & 31)
            spread_counts(hist.astype(F32), groups, mult_ref, a)
        for q, group in enumerate([highs[:4], highs[4:], lows[:4], lows[4:]]):
            at = width + 16 * q
            pk[at : at + 16, :] = narrow(jnp.concatenate(group, 1))

        slab_t = et0_ref if first else et_ref
        slab_t[...] = slab[...].T

        def left_hot(n, carry):
            at = n * chunk
            oh_ref[pl.ds(at, chunk), :] = one_hot(left_row, n * chunk, (chunk, slots))
            return carry

        def right_hot(n, carry):
            at = n * chunk
            oh_ref[pl.ds(at, chunk), :] = one_hot(right_row, n * chunk, (chunk, slots))
            return carry

        loop(chunks, left_hot, 0)
        left_t = dot(et0_ref[...], oh_ref[...]).astype(BF)
        if at_call == 0:
            ops_copy.wait()
        query_t = jnp.concatenate(
            [dot(ops_ref[i], left_t[:, 128 * i : 128 * (i + 1)], TN) for i in range(rel_own)], 1
        ).astype(BF)
        pk[0:width, :] = query_t
        half_t = query_t * 0.5
        loop(chunks, right_hot, 0)
        right_t = dot(slab_t[...], oh_ref[...])
        positive = jnp.sum(query_t.astype(F32) * right_t, axis=0, keepdims=True)
        pos_grad = -live * jax.nn.sigmoid(-positive)
        pos_high = pos_grad.astype(BF)
        pos_low = (pos_grad - pos_high.astype(F32)).astype(BF)
        misc = [narrow(parts[2]), narrow(parts[3]), narrow(live), pos_high, pos_low]
        misc = [row.astype(F32) for row in misc] + [jnp.zeros((11, slots), F32)]
        pk[width + 64 : width + 80, :] = jnp.concatenate(misc, 0).astype(BF)
        if first:
            pk_copy.start()
        factor = live * (0.5 * neg_scale)

        def weigh(n, carry):
            at = n * chunk
            level = jnp.tanh(dot(slab[pl.ds(at, chunk), :], half_t))
            ngrad = (level * factor + factor).astype(BF).astype(F32)
            mult = mult_ref[pl.ds(at, chunk), :]
            weight = ngrad * jnp.concatenate([mult] * rel_own, 1)
            high = weight.astype(BF)
            whi_ref[pl.ds(at, chunk), :] = high
            wlo_ref[pl.ds(at, chunk), :] = (weight - high.astype(F32)).astype(BF)
            return carry

        loop(chunks, weigh, 0)
        qgrad_t = dot(slab_t[...], whi_ref[...]) + dot(slab_t[...], wlo_ref[...])
        qgrad_t = (qgrad_t + right_t * pos_grad).astype(BF)
        qg_ref[at_call] = qgrad_t
        qg_copies[at_call].start()
        for i in range(rel_own):
            cols = slice(128 * i, 128 * (i + 1))
            outer = dot(left_t[:, cols], qgrad_t[:, cols], NT)
            if first:
                rel_acc[i] = outer
            elif at_call == 0:
                rel_acc[i] = sum_ref[i] + outer
            else:
                rel_acc[i] = rel_acc[i] + outer

    if first:
        pk_copy.wait()
        qg_copies[0].wait()
        return
    doms, held, _ = rel_ref.shape
    held = held // rel_own
    for d in range(doms):
        block = [rel_acc[i, held * d : held * (d + 1), :] for i in range(rel_own)]
        rel_ref[d] = jnp.concatenate(block, 0).astype(BF)
    for copy in qg_copies:
        copy.wait()


def entity_kernel(buckets, neg_scale, groups, me_ref, slab_ref, ops_hbm, *refs):
    lrow0_ref, lrow_ref = refs[:2]
    qg_hbms, pk_refs = refs[2 : 2 + buckets], list(refs[2 + buckets : 2 + 2 * buckets])
    keep_ref, send_ref, rows_ref, mult_ref, ops_ref, qg_ref, pk_ref, sems = refs[2 + 2 * buckets :]
    copies = [
        pltpu.make_async_copy(pk_refs[0], pk_ref, sems.at[0]),
        pltpu.make_async_copy(ops_hbm, ops_ref, sems.at[1]),
    ]
    for s in range(buckets):
        copies.append(pltpu.make_async_copy(qg_hbms[s], qg_ref.at[s], sems.at[2 + s]))
    for copy in copies:
        copy.start()
    pk_refs[0] = pk_ref
    me = me_ref[0]
    rel_own, width, _ = ops_hbm.shape
    part_rows = slab_ref.shape[0]
    slots = rel_own * 128
    chunk = 256
    chunks = part_rows // chunk
    share = part_rows // groups
    for step, s in enumerate(list(range(1, buckets)) + [0]):
        pk = pk_refs[s]
        if s == 0:
            copies[0].wait()
        hist = pk[width : width + 64, :].astype(F32)
        hist = hist[:32] * 32.0 + hist[32:]
        for a in range(8):
            cols = slice(128 * (a % 4), 128 * (a % 4 + 1))
            spread_counts(hist[16 * (a // 4) : 16 * (a // 4 + 1), cols], groups, mult_ref, a)
        misc = pk[width + 64 : width + 80, :].astype(F32)
        right_row = (misc[0:1] * 32.0 + misc[1:2]).astype(jnp.int32)
        factor = misc[2:3] * (0.5 * neg_scale)
        pos_grad = misc[3:4] + misc[4:5]
        query_t = pk[0:width, :]
        half_t = query_t * 0.5

        def weigh(n, carry):
            at = n * chunk
            level = jnp.tanh(dot(slab_ref[pl.ds(at, chunk), :], half_t))
            ngrad = (level * factor + factor).astype(BF).astype(F32)
            mult = mult_ref[pl.ds(at, chunk), :]
            hit = (iota((chunk, slots), 0) + n * chunk) == right_row
            weight = ngrad * jnp.concatenate([mult] * rel_own, 1) + jnp.where(hit, pos_grad, 0.0)
            high = weight.astype(BF)
            low = (weight - high.astype(F32)).astype(BF)
            rows = dot(high, query_t, NT) + dot(low, query_t, NT)
            rows_ref[pl.ds(at, chunk), :] = rows if step == 0 else rows_ref[pl.ds(at, chunk), :] + rows
            return carry

        loop(chunks, weigh, 0)
    for copy in copies[1:]:
        copy.wait()
    lefts = [lrow0_ref[0:1, :]] + [lrow_ref[s - 1 : s, :] for s in range(1, buckets)]
    grads = []
    for s in range(buckets):
        qgrad_t = qg_ref[s]
        for i in range(rel_own):
            grads.append(dot(ops_ref[i], qgrad_t[:, 128 * i : 128 * (i + 1)]).astype(BF))
    lgrad_t = jnp.concatenate(grads, 1)
    for n in range(chunks):
        hot = [one_hot(left, n * chunk, (chunk, slots)) for left in lefts]
        rows_ref[pl.ds(n * chunk, chunk), :] += dot(jnp.concatenate(hot, 1), lgrad_t, NT)
    for n in range(groups):
        to = me ^ (((n >> 1) & 3) * 4 + (n & 1) * 2 + (n >> 3))
        block = rows_ref[pl.ds(pl.multiple_of(to * share, share), share), :]
        half = groups // 2
        if n < half:
            keep_ref[n] = block
        else:
            send_ref[n - half] = block


def finish_kernel(keep_ref, got_ref, parts_ref, ent_ref, rel_ref):
    ent_ref[...] = keep_ref[...] + got_ref[...]
    total = parts_ref[0].astype(F32)
    for n in range(1, parts_ref.shape[0]):
        total = total + parts_ref[n].astype(F32)
    rel_ref[...] = total


def shards(entities, operators, left_rows, right_rows, negatives, counts):
    buckets = left_rows.shape[0]
    slot_count = left_rows.shape[-1]
    neg_count = negatives.shape[-1]
    groups = lax.axis_size("span")
    doms = lax.axis_size("dom")
    rel_own = operators.shape[0]
    relations = rel_own * groups
    part_rows, width = entities.shape
    neg_scale = float(neg_count) ** (-0.5)
    share = part_rows // groups
    slots = rel_own * 128
    limit = pltpu.CompilerParams(vmem_limit_bytes=12 * 1024 * 1024)
    small = pltpu.CompilerParams(vmem_limit_bytes=2 * 1024 * 1024)

    packed = pl.pallas_call(
        functools.partial(pack_kernel, groups),
        out_shape=jax.ShapeDtypeStruct((groups, 16, 128), jnp.int32),
        in_specs=[VMEM] * 4,
        out_specs=VMEM,
        name="pack_lists",
    )(
        negatives.reshape(buckets, neg_count // 128, 128),
        left_rows.reshape(buckets, slot_count // 128, 128),
        right_rows.reshape(buckets, slot_count // 128, 128),
        counts.reshape(buckets, 1, relations),
    )
    received = exchanged(packed, "span")
    near = shifted(entities, -1, -2)
    near = pl.pallas_call(
        tie_kernel,
        out_shape=jax.ShapeDtypeStruct(entities.shape, BF),
        in_specs=[VMEM, VMEM],
        out_specs=VMEM,
        compiler_params=small,
        name="after_lists",
    )(near, received)
    slabs = [near, swapped(near, 1)]

    me = lax.axis_index("span").astype(jnp.int32).reshape(1)
    wide = pltpu.VMEM((part_rows, slots), BF)

    def scratch_of(many):
        return [
            wide,
            wide,
            wide,
            pltpu.VMEM((part_rows, 128), F32),
            pltpu.VMEM(operators.shape, BF),
            pltpu.VMEM((many, width, slots), BF),
            pltpu.SemaphoreType.DMA,
            pltpu.SemaphoreType.DMA((many,)),
        ]

    def packs_of(many, pack):
        return (
            [jax.ShapeDtypeStruct((8, slots), jnp.int32)]
            + [pltpu.HBM((width, slots), BF)] * many
            + [pack((width + 80, slots), BF)] * many
        )

    rel_sum, slab_t, lrow_own, qg_own, pack_own = pl.pallas_call(
        functools.partial(forward_kernel, buckets, (0,), neg_scale),
        out_shape=[
            jax.ShapeDtypeStruct((rel_own, width, width), F32),
            jax.ShapeDtypeStruct((width, part_rows), BF),
        ]
        + packs_of(1, pltpu.HBM),
        in_specs=[SMEM, VMEM, VMEM, HBM],
        out_specs=[VMEM] * 3 + [HBM] * 2,
        scratch_shapes=scratch_of(1)
        + [pltpu.VMEM((width + 80, slots), BF), pltpu.SemaphoreType.DMA],
        compiler_params=limit,
        cost_estimate=pl.CostEstimate(
            flops=1_400_000_000, bytes_accessed=2_000_000, transcendentals=500_000
        ),
        name="own_bucket",
    )(me, received, entities, operators)
    others = tuple(range(1, buckets))
    rel_parts, lrow_other, *packs = pl.pallas_call(
        functools.partial(forward_kernel, buckets, others, neg_scale),
        out_shape=[jax.ShapeDtypeStruct((doms, rel_own * width // doms, width), BF)]
        + packs_of(buckets - 1, jax.ShapeDtypeStruct),
        in_specs=[SMEM] + [VMEM] * buckets + [HBM, VMEM, VMEM],
        out_specs=[VMEM] * 2 + [HBM] * (buckets - 1) + [VMEM] * (buckets - 1),
        scratch_shapes=scratch_of(buckets - 1)
        + [pltpu.VMEM((rel_own, width, width), F32), pltpu.VMEM((width, part_rows), BF)],
        compiler_params=limit,
        cost_estimate=pl.CostEstimate(
            flops=3_000_000_000, bytes_accessed=3_000_000, transcendentals=1_100_000
        ),
        name="other_buckets",
    )(me, received, *slabs, operators, slab_t, rel_sum)
    pack_own = pltpu.with_memory_space_constraint(pack_own, pltpu.HBM)
    grads = [pltpu.with_memory_space_constraint(grad, pltpu.HBM) for grad in [qg_own] + packs[:2]]
    packs = [pack_own, shifted(packs[2], 1, 2), shifted(packs[3], 2, 1)]
    rel_arrived = exchanged(rel_parts, "dom")

    half_parts = jax.ShapeDtypeStruct((groups // 2, share, width), F32)
    keep, send = pl.pallas_call(
        functools.partial(entity_kernel, buckets, neg_scale, groups),
        out_shape=(half_parts, half_parts),
        in_specs=[SMEM, VMEM, HBM, VMEM, VMEM] + [HBM] * (buckets + 1) + [VMEM] * (buckets - 1),
        out_specs=(VMEM, VMEM),
        scratch_shapes=[
            pltpu.VMEM((part_rows, width), F32),
            pltpu.VMEM((part_rows, 128), F32),
            pltpu.VMEM(operators.shape, BF),
            pltpu.VMEM((buckets, width, slots), BF),
            pltpu.VMEM((width + 80, slots), BF),
            pltpu.SemaphoreType.DMA((buckets + 2,)),
        ],
        compiler_params=limit,
        cost_estimate=pl.CostEstimate(
            flops=4_000_000_000, bytes_accessed=3_000_000, transcendentals=1_600_000
        ),
        name="entity_gradients",
    )(me, entities, operators, lrow_own, lrow_other, *grads, *packs)

    total = keep + swapped(send, 1)
    total = total.reshape(4, 2, share, width)
    got = [swapped(total[x].astype(BF), 4 * x) for x in (1, 2, 3)]
    total = total[0] + sum(part.astype(F32) for part in got)
    held = rel_own * width // doms
    entity_share, rel_share = pl.pallas_call(
        finish_kernel,
        out_shape=(
            jax.ShapeDtypeStruct((share, width), F32),
            jax.ShapeDtypeStruct((held, width), F32),
        ),
        in_specs=[VMEM] * 3,
        out_specs=(VMEM, VMEM),
        compiler_params=small,
        name="last_sums",
    )(total[0], swapped(total[1], 2), rel_arrived)
    return (entity_share, rel_share.reshape(rel_own, width // doms, width))


def solution(mesh):
    in_specs = (
        P("dom", None),
        P("span", None, None),
        P(None, "dom", "span", None),
        P(None, "dom", "span", None),
        P(None, "dom", "span", None),
        P(None, "dom", "span", None),
    )
    out_specs = (P(("dom", "span"), None), P("span", "dom", None))
    return jax.shard_map(shards, mesh=mesh, in_specs=in_specs, out_specs=out_specs, check_vma=False)
```

```python
import functools

import jax
import jax.numpy as jnp
from jax import lax
from jax.experimental import pallas as pl
from jax.experimental.pallas import tpu as pltpu
from jax.sharding import PartitionSpec as P

BF = jnp.bfloat16
F32 = jnp.float32
NT = (((1,), (1,)), ((), ()))
TN = (((0,), (0,)), ((), ()))
VMEM = pl.BlockSpec(memory_space=pltpu.VMEM)
SMEM = pl.BlockSpec(memory_space=pltpu.SMEM)
HBM = pl.BlockSpec(memory_space=pltpu.HBM)


def dot(a, b, dims=(((1,), (0,)), ((), ()))):
    return lax.dot_general(a, b, dims, preferred_element_type=F32)


def shifted(value, step, other):
    doms, groups = lax.axis_size("dom"), lax.axis_size("span")
    pairs = []
    for p in range(doms):
        for c in range(groups):
            to = (p + (other if c & 1 else step)) % doms
            pairs.append((p * groups + c, to * groups + c))
    return lax.ppermute(value, ("dom", "span"), pairs)


def swapped(value, bits):
    groups = lax.axis_size("span")
    return lax.ppermute(value, "span", [(i, i ^ bits) for i in range(groups)])


def exchanged(value, axis):
    return lax.all_to_all(value, axis, split_axis=0, concat_axis=0, tiled=True)


def iota(shape, axis):
    return lax.broadcasted_iota(jnp.int32, shape, axis)


def pack_kernel(groups, neg_ref, left_ref, right_ref, count_ref, out_ref):
    hists = []
    for s in range(3):
        high, low = [], []
        for q in range(neg_ref.shape[1]):
            row = neg_ref[s, q : q + 1, :]
            high.append((iota((16, 128), 0) == (row >> 7)).astype(F32).astype(BF))
            low.append((iota((128, 128), 0) == (row & 127)).astype(F32).astype(BF))
        hist = dot(jnp.concatenate(high, 1), jnp.concatenate(low, 1), NT)[:8]
        hists.append(hist.astype(jnp.int32))
    words = hists[0] + (hists[1] << 16)
    for d in range(groups):
        out_ref[d, 0:8, :] = words
    lines = left_ref.shape[1]
    counts = [count_ref[s] for s in range(3)]
    counts = counts + [jnp.zeros(counts[0].shape, jnp.int32)]
    counts = [jnp.concatenate(counts[:2], 1), jnp.concatenate(counts[2:], 1)]
    for line in range(lines):
        rows = [ref[s, line : line + 1, :] for ref in (left_ref, right_ref) for s in range(3)]
        words = hists[2] + (jnp.concatenate(rows + counts, 0) << 16)
        for d in range(line * groups // lines, (line + 1) * groups // lines):
            out_ref[d, 8:16, :] = words


def loop(n, step, carry):
    for i in range(n):
        carry = step(i, carry)
    return carry


def tie_kernel(held_ref, first_ref, out_ref):
    out_ref[...] = held_ref[...]


def one_hot(rows, at, shape):
    return ((iota(shape, 0) + at) == rows).astype(F32).astype(BF)


def spread_counts(hist, groups, mult_ref, a):
    hist = jnp.broadcast_to(hist[:, None, :], (groups, 8, 128)).reshape(128, 128)
    mult_ref[128 * a : 128 * (a + 1), :] = hist.T


def forward_kernel(turn, neg_scale, *refs):
    first, last = turn == 0, turn == 2
    olds = (0, 2, 1)[turn]
    me_ref, x_ref, slab, ops_hbm = refs[:4]
    refs = refs[4:]
    if not first:
        et0_ref, sum_ref = refs[:2]
        refs = refs[2:]
    old_refs, refs = refs[:olds], refs[olds:]
    if first:
        et0_ref, rel_acc = refs[:2]
        refs = refs[2:]
    elif last:
        rel_ref, refs = refs[0], refs[1:]
    else:
        rel_acc, refs = refs[0], refs[1:]
    lrow_ref, qg_ref, pk = refs[:3]
    old_hbms, refs = refs[3 : 3 + olds], refs[3 + olds :]
    oh_ref, whi_ref, wlo_ref, mult_ref, ops_ref, et_ref, ops_sem, old_sems = refs[:8]
    if last:
        rel_acc, qg_hbm, qg_ref, qg_sem = refs[8], qg_ref, refs[9], refs[10]
    ops_copy = pltpu.make_async_copy(ops_hbm, ops_ref, ops_sem)
    ops_copy.start()
    old_copies = [
        pltpu.make_async_copy(old_refs[n], old_hbms[n], old_sems.at[n]) for n in range(olds)
    ]
    for copy in old_copies:
        copy.start()
    rel_own, width, _ = ops_hbm.shape
    groups = x_ref.shape[0]
    part_rows = slab.shape[0]
    slots = rel_own * 128
    chunk = 256
    chunks = part_rows // chunk
    me = me_ref[0]
    core = me & 1

    lane_row = iota((128, slots), 0)
    lane = iota((128, slots), 1)
    relation, slot = lane >> 7, lane & 7
    per_line = 128 // (8 * rel_own)
    pick_slot = (lane_row == (me % per_line) * (8 * rel_own) + relation * 8 + slot)
    pick_slot = pick_slot.astype(F32).astype(BF)
    count_lane = me * rel_own + relation
    lane = iota((groups, slots), 1)
    own_group = iota((groups, slots), 0) == ((lane >> 3) & (groups - 1))
    slot_row = iota((1, slots), 1) & 7

    def own(values):
        return jnp.sum(jnp.where(own_group, values, 0.0), axis=0, keepdims=True)

    def narrow(values):
        return values.astype(F32).astype(BF)

    s = (0, 1 + core, 2 - core)[turn]
    left, right = x_ref[:, 8 + s, :] >> 16, x_ref[:, 11 + s, :] >> 16
    parts = [left >> 5, left & 31, right >> 5, right & 31]
    parts = dot(narrow(jnp.concatenate(parts, 0)), pick_slot)
    parts = [own(parts[groups * q : groups * (q + 1)]) for q in range(4)]
    left_row = (parts[0] * 32.0 + parts[1]).astype(jnp.int32)
    right_row = (parts[2] * 32.0 + parts[3]).astype(jnp.int32)
    pick_count = narrow(lane_row == count_lane + (s % 2) * (groups * rel_own))
    count_row = own(dot(narrow(x_ref[:, 14 + s // 2, :] >> 16), pick_count))
    live = (count_row.astype(jnp.int32) > slot_row).astype(F32)
    lrow_ref[0:1, :] = left_row

    highs, lows = [], []
    for a in range(8):
        hist = (x_ref[:, (s // 2) * 8 + a, :] >> (16 * (s % 2))) & 65535
        highs.append(hist >> 5)
        lows.append(hist & 31)
        spread_counts(hist.astype(F32), groups, mult_ref, a)
    for q, group in enumerate([highs[:4], highs[4:], lows[:4], lows[4:]]):
        at = width + 16 * q
        pk[at : at + 16, :] = narrow(jnp.concatenate(group, 1))

    slab_t = et0_ref if first else et_ref
    slab_t[...] = slab[...].T

    def left_hot(n, carry):
        at = n * chunk
        oh_ref[pl.ds(at, chunk), :] = one_hot(left_row, n * chunk, (chunk, slots))
        return carry

    def right_hot(n, carry):
        at = n * chunk
        oh_ref[pl.ds(at, chunk), :] = one_hot(right_row, n * chunk, (chunk, slots))
        return carry

    loop(chunks, left_hot, 0)
    left_t = dot(et0_ref[...], oh_ref[...]).astype(BF)
    ops_copy.wait()
    query_t = jnp.concatenate(
        [dot(ops_ref[i], left_t[:, 128 * i : 128 * (i + 1)], TN) for i in range(rel_own)], 1
    ).astype(BF)
    pk[0:width, :] = query_t
    half_t = query_t * 0.5
    loop(chunks, right_hot, 0)
    right_t = dot(slab_t[...], oh_ref[...])
    positive = jnp.sum(query_t.astype(F32) * right_t, axis=0, keepdims=True)
    pos_grad = -live * jax.nn.sigmoid(-positive)
    pos_high = pos_grad.astype(BF)
    pos_low = (pos_grad - pos_high.astype(F32)).astype(BF)
    misc = [narrow(parts[2]), narrow(parts[3]), narrow(live), pos_high, pos_low]
    misc = [row.astype(F32) for row in misc] + [jnp.zeros((11, slots), F32)]
    pk[width + 64 : width + 80, :] = jnp.concatenate(misc, 0).astype(BF)
    factor = live * (0.5 * neg_scale)

    def weigh(n, carry):
        at = n * chunk
        level = jnp.tanh(dot(slab[pl.ds(at, chunk), :], half_t))
        ngrad = (level * factor + factor).astype(BF).astype(F32)
        mult = mult_ref[pl.ds(at, chunk), :]
        weight = ngrad * jnp.concatenate([mult] * rel_own, 1)
        high = weight.astype(BF)
        whi_ref[pl.ds(at, chunk), :] = high
        wlo_ref[pl.ds(at, chunk), :] = (weight - high.astype(F32)).astype(BF)
        return carry

    loop(chunks, weigh, 0)
    qgrad_t = dot(slab_t[...], whi_ref[...]) + dot(slab_t[...], wlo_ref[...])
    qgrad_t = (qgrad_t + right_t * pos_grad).astype(BF)
    qg_ref[...] = qgrad_t
    if last:
        qg_copy = pltpu.make_async_copy(qg_ref, qg_hbm, qg_sem)
        qg_copy.start()
    for i in range(rel_own):
        cols = slice(128 * i, 128 * (i + 1))
        outer = dot(left_t[:, cols], qgrad_t[:, cols], NT)
        rel_acc[i] = outer if first else sum_ref[i] + outer

    for copy in old_copies:
        copy.wait()
    if not last:
        return
    doms, held, _ = rel_ref.shape
    held = held // rel_own
    for d in range(doms):
        block = [rel_acc[i, held * d : held * (d + 1), :] for i in range(rel_own)]
        rel_ref[d] = jnp.concatenate(block, 0).astype(BF)
    qg_copy.wait()


def right_rows_added(neg_scale, groups, pk, slab_ref, mult_ref, rows_ref, before):
    part_rows, width = slab_ref.shape
    slots = pk.shape[1]
    chunk = 256
    hist = pk[width : width + 64, :].astype(F32)
    hist = hist[:32] * 32.0 + hist[32:]
    for a in range(8):
        cols = slice(128 * (a % 4), 128 * (a % 4 + 1))
        spread_counts(hist[16 * (a // 4) : 16 * (a // 4 + 1), cols], groups, mult_ref, a)
    misc = pk[width + 64 : width + 80, :].astype(F32)
    right_row = (misc[0:1] * 32.0 + misc[1:2]).astype(jnp.int32)
    factor = misc[2:3] * (0.5 * neg_scale)
    pos_grad = misc[3:4] + misc[4:5]
    query_t = pk[0:width, :]
    half_t = query_t * 0.5
    for n in range(part_rows // chunk):
        at = pl.ds(n * chunk, chunk)
        level = jnp.tanh(dot(slab_ref[at, :], half_t))
        ngrad = (level * factor + factor).astype(BF).astype(F32)
        mult = mult_ref[at, :]
        hit = (iota((chunk, slots), 0) + n * chunk) == right_row
        weight = ngrad * jnp.concatenate([mult] * (slots // 128), 1)
        weight = weight + jnp.where(hit, pos_grad, 0.0)
        high = weight.astype(BF)
        low = (weight - high.astype(F32)).astype(BF)
        rows = dot(high, query_t, NT) + dot(low, query_t, NT)
        rows_ref[at, :] = rows if before is None else before[at, :] + rows


def entity_kernel(neg_scale, groups, slab_ref, ops_hbm, *refs):
    lrow_refs, qg_hbms, pk_hbm, pk_other = refs[:3], refs[3:6], refs[6], refs[7]
    rows_ref, mult_ref, ops_ref, qg_ref, pk_ref, sems = refs[8:]
    copies = [
        pltpu.make_async_copy(pk_hbm, pk_ref, sems.at[0]),
        pltpu.make_async_copy(ops_hbm, ops_ref, sems.at[1]),
    ]
    for s in range(3):
        copies.append(pltpu.make_async_copy(qg_hbms[s], qg_ref.at[s], sems.at[2 + s]))
    for copy in copies:
        copy.start()
    rel_own = ops_hbm.shape[0]
    part_rows = slab_ref.shape[0]
    slots = rel_own * 128
    chunk = 256
    right_rows_added(neg_scale, groups, pk_other, slab_ref, mult_ref, rows_ref, None)
    copies[0].wait()
    right_rows_added(neg_scale, groups, pk_ref, slab_ref, mult_ref, rows_ref, rows_ref)
    for copy in copies[1:]:
        copy.wait()
    grads = []
    for s in range(3):
        qgrad_t = qg_ref[s]
        for i in range(rel_own):
            grads.append(dot(ops_ref[i], qgrad_t[:, 128 * i : 128 * (i + 1)]).astype(BF))
    lgrad_t = jnp.concatenate(grads, 1)
    for n in range(part_rows // chunk):
        hot = [one_hot(ref[0:1, :], n * chunk, (chunk, slots)) for ref in lrow_refs]
        rows_ref[pl.ds(n * chunk, chunk), :] += dot(jnp.concatenate(hot, 1), lgrad_t, NT)


def last_entity_kernel(
    neg_scale, groups, me_ref, slab_ref, pk, before, keep_ref, send_ref, rows_ref, mult_ref
):
    right_rows_added(neg_scale, groups, pk, slab_ref, mult_ref, rows_ref, before)
    me = me_ref[0]
    share = slab_ref.shape[0] // groups
    half = groups // 2
    for n in range(groups):
        to = me ^ (((n >> 1) & 3) * 4 + (n & 1) * 2 + (n >> 3))
        block = rows_ref[pl.ds(pl.multiple_of(to * share, share), share), :]
        if n < half:
            keep_ref[n] = block
        else:
            send_ref[n - half] = block


def finish_kernel(keep_ref, got_ref, parts_ref, ent_ref, rel_ref):
    ent_ref[...] = keep_ref[...] + got_ref[...]
    total = parts_ref[0].astype(F32)
    for n in range(1, parts_ref.shape[0]):
        total = total + parts_ref[n].astype(F32)
    rel_ref[...] = total


def shards(entities, operators, left_rows, right_rows, negatives, counts):
    buckets = left_rows.shape[0]
    slot_count = left_rows.shape[-1]
    neg_count = negatives.shape[-1]
    groups = lax.axis_size("span")
    doms = lax.axis_size("dom")
    rel_own = operators.shape[0]
    relations = rel_own * groups
    part_rows, width = entities.shape
    neg_scale = float(neg_count) ** (-0.5)
    share = part_rows // groups
    slots = rel_own * 128
    limit = pltpu.CompilerParams(vmem_limit_bytes=12 * 1024 * 1024)
    small = pltpu.CompilerParams(vmem_limit_bytes=2 * 1024 * 1024)

    packed = pl.pallas_call(
        functools.partial(pack_kernel, groups),
        out_shape=jax.ShapeDtypeStruct((groups, 16, 128), jnp.int32),
        in_specs=[VMEM] * 4,
        out_specs=VMEM,
        name="pack_lists",
    )(
        negatives.reshape(buckets, neg_count // 128, 128),
        left_rows.reshape(buckets, slot_count // 128, 128),
        right_rows.reshape(buckets, slot_count // 128, 128),
        counts.reshape(buckets, 1, relations),
    )
    received = exchanged(packed, "span")
    near = shifted(entities, -1, -2)
    near = pl.pallas_call(
        tie_kernel,
        out_shape=jax.ShapeDtypeStruct(entities.shape, BF),
        in_specs=[VMEM, VMEM],
        out_specs=VMEM,
        compiler_params=small,
        name="after_lists",
    )(near, received)
    slabs = [near, swapped(near, 1)]

    me = lax.axis_index("span").astype(jnp.int32).reshape(1)
    wide = pltpu.VMEM((part_rows, slots), BF)

    packed_shape = (width + 80, slots)
    grad_shape = (width, slots)
    sums = jax.ShapeDtypeStruct((rel_own, width, width), F32)

    def forward(turn, slab, before, olds):
        last = turn == 2
        outs = [jax.ShapeDtypeStruct((width, part_rows), BF)] if turn == 0 else []
        relation_parts = jax.ShapeDtypeStruct((doms, rel_own * width // doms, width), BF)
        outs.append(relation_parts if last else sums)
        outs.append(jax.ShapeDtypeStruct((8, slots), jnp.int32))
        specs = [VMEM] * len(outs)
        outs.append(pltpu.HBM(grad_shape, BF) if last else jax.ShapeDtypeStruct(grad_shape, BF))
        specs.append(HBM if last else VMEM)
        outs.append(jax.ShapeDtypeStruct(packed_shape, BF))
        specs.append(VMEM)
        outs += [pltpu.HBM(old.shape, BF) for old in olds]
        specs += [HBM] * len(olds)
        scratch = [
            wide,
            wide,
            wide,
            pltpu.VMEM((part_rows, 128), F32),
            pltpu.VMEM(operators.shape, BF),
            pltpu.VMEM((width, part_rows), BF),
            pltpu.SemaphoreType.DMA,
            pltpu.SemaphoreType.DMA((2,)),
        ]
        if last:
            scratch += [
                pltpu.VMEM((rel_own, width, width), F32),
                pltpu.VMEM(grad_shape, BF),
                pltpu.SemaphoreType.DMA,
            ]
        return pl.pallas_call(
            functools.partial(forward_kernel, turn, neg_scale),
            out_shape=outs,
            in_specs=[SMEM, VMEM, VMEM, HBM] + [VMEM] * (len(before) + len(olds)),
            out_specs=specs,
            scratch_shapes=scratch,
            compiler_params=limit,
            cost_estimate=pl.CostEstimate(
                flops=1_450_000_000, bytes_accessed=2_000_000, transcendentals=500_000
            ),
            name=("own_bucket", "near_bucket", "far_bucket")[turn],
        )(me, received, slab, operators, *before, *olds)

    slab_t, rel_sum, lrow_0, qg_0, pack_0 = forward(0, entities, (), ())
    rel_sum, lrow_1, qg_1, pack_1, pack_0, qg_0 = forward(
        1, slabs[0], (slab_t, rel_sum), (pack_0, qg_0)
    )
    pack_1 = shifted(pack_1, 1, 2)
    rel_parts, lrow_2, qg_2, pack_2, qg_1 = forward(2, slabs[1], (slab_t, rel_sum), (qg_1,))
    pack_2 = shifted(pack_2, 2, 1)
    rel_arrived = exchanged(rel_parts, "dom")

    hold = functools.partial(pltpu.with_memory_space_constraint, memory_space=pltpu.HBM)
    rows = pl.pallas_call(
        functools.partial(entity_kernel, neg_scale, groups),
        out_shape=jax.ShapeDtypeStruct((part_rows, width), F32),
        in_specs=[VMEM, HBM] + [VMEM] * 3 + [HBM] * 4 + [VMEM],
        out_specs=VMEM,
        scratch_shapes=[
            pltpu.VMEM((part_rows, 128), F32),
            pltpu.VMEM(operators.shape, BF),
            pltpu.VMEM((3,) + grad_shape, BF),
            pltpu.VMEM(packed_shape, BF),
            pltpu.SemaphoreType.DMA((5,)),
        ],
        compiler_params=limit,
        cost_estimate=pl.CostEstimate(
            flops=3_000_000_000, bytes_accessed=3_000_000, transcendentals=1_000_000
        ),
        name="entity_gradients",
    )(
        entities,
        operators,
        lrow_0,
        lrow_1,
        lrow_2,
        hold(qg_0),
        hold(qg_1),
        hold(qg_2),
        hold(pack_0),
        pack_1,
    )
    half_parts = jax.ShapeDtypeStruct((groups // 2, share, width), F32)
    keep, send = pl.pallas_call(
        functools.partial(last_entity_kernel, neg_scale, groups),
        out_shape=(half_parts, half_parts),
        in_specs=[SMEM] + [VMEM] * 3,
        out_specs=(VMEM, VMEM),
        scratch_shapes=[
            pltpu.VMEM((part_rows, width), F32),
            pltpu.VMEM((part_rows, 128), F32),
        ],
        compiler_params=limit,
        cost_estimate=pl.CostEstimate(
            flops=1_000_000_000, bytes_accessed=2_000_000, transcendentals=500_000
        ),
        name="last_entity_gradients",
    )(me, entities, pack_2, rows)

    total = keep + swapped(send, 1)
    total = total.reshape(4, 2, share, width)
    got = [swapped(total[x].astype(BF), 4 * x) for x in (1, 2, 3)]
    total = total[0] + sum(part.astype(F32) for part in got)
    held = rel_own * width // doms
    entity_share, rel_share = pl.pallas_call(
        finish_kernel,
        out_shape=(
            jax.ShapeDtypeStruct((share, width), F32),
            jax.ShapeDtypeStruct((held, width), F32),
        ),
        in_specs=[VMEM] * 3,
        out_specs=(VMEM, VMEM),
        compiler_params=small,
        name="last_sums",
    )(total[0], swapped(total[1], 2), rel_arrived)
    return (entity_share, rel_share.reshape(rel_own, width // doms, width))


def solution(mesh):
    in_specs = (
        P("dom", None),
        P("span", None, None),
        P(None, "dom", "span", None),
        P(None, "dom", "span", None),
        P(None, "dom", "span", None),
        P(None, "dom", "span", None),
    )
    out_specs = (P(("dom", "span"), None), P("span", "dom", None))
    return jax.shard_map(shards, mesh=mesh, in_specs=in_specs, out_specs=out_specs, check_vma=False)
```

```python
import functools

import jax
import jax.numpy as jnp
from jax import lax
from jax.experimental import pallas as pl
from jax.experimental.pallas import tpu as pltpu
from jax.sharding import PartitionSpec as P

BF = jnp.bfloat16
F32 = jnp.float32
NT = (((1,), (1,)), ((), ()))
TN = (((0,), (0,)), ((), ()))
VMEM = pl.BlockSpec(memory_space=pltpu.VMEM)
SMEM = pl.BlockSpec(memory_space=pltpu.SMEM)
HBM = pl.BlockSpec(memory_space=pltpu.HBM)


def dot(a, b, dims=(((1,), (0,)), ((), ()))):
    return lax.dot_general(a, b, dims, preferred_element_type=F32)


def shifted(value, step, other):
    doms, groups = lax.axis_size("dom"), lax.axis_size("span")
    pairs = []
    for p in range(doms):
        for c in range(groups):
            to = (p + (other if c & 1 else step)) % doms
            pairs.append((p * groups + c, to * groups + c))
    return lax.ppermute(value, ("dom", "span"), pairs)


def swapped(value, bits):
    groups = lax.axis_size("span")
    return lax.ppermute(value, "span", [(i, i ^ bits) for i in range(groups)])


def exchanged(value, axis):
    return lax.all_to_all(value, axis, split_axis=0, concat_axis=0, tiled=True)


def iota(shape, axis):
    return lax.broadcasted_iota(jnp.int32, shape, axis)


def pack_kernel(groups, neg_ref, left_ref, right_ref, count_ref, out_ref):
    hists = []
    for s in range(3):
        high, low = [], []
        for q in range(neg_ref.shape[1]):
            row = neg_ref[s, q : q + 1, :]
            high.append((iota((16, 128), 0) == (row >> 7)).astype(F32).astype(BF))
            low.append((iota((128, 128), 0) == (row & 127)).astype(F32).astype(BF))
        hist = dot(jnp.concatenate(high, 1), jnp.concatenate(low, 1), NT)[:8]
        hists.append(hist.astype(jnp.int32))
    words = hists[0] + (hists[1] << 16)
    for d in range(groups):
        out_ref[d, 0:8, :] = words
    lines = left_ref.shape[1]
    counts = [count_ref[s] for s in range(3)]
    counts = counts + [jnp.zeros(counts[0].shape, jnp.int32)]
    counts = [jnp.concatenate(counts[:2], 1), jnp.concatenate(counts[2:], 1)]
    for line in range(lines):
        rows = [ref[s, line : line + 1, :] for ref in (left_ref, right_ref) for s in range(3)]
        words = hists[2] + (jnp.concatenate(rows + counts, 0) << 16)
        for d in range(line * groups // lines, (line + 1) * groups // lines):
            out_ref[d, 8:16, :] = words


def loop(n, step, carry):
    for i in range(n):
        carry = step(i, carry)
    return carry


def tie_kernel(held_ref, first_ref, out_ref):
    out_ref[...] = held_ref[...]


def one_hot(rows, at, shape):
    return ((iota(shape, 0) + at) == rows).astype(F32).astype(BF)


def spread_counts(hist, groups, mult_ref, a):
    hist = jnp.broadcast_to(hist[:, None, :], (groups, 8, 128)).reshape(128, 128)
    mult_ref[128 * a : 128 * (a + 1), :] = hist.T


def forward_kernel(turn, neg_scale, *refs):
    first, last = turn == 0, turn == 2
    olds = (0, 2, 1)[turn]
    me_ref, x_ref, slab, ops_hbm = refs[:4]
    refs = refs[4:]
    if not first:
        et0_ref, sum_ref = refs[:2]
        refs = refs[2:]
    old_refs, refs = refs[:olds], refs[olds:]
    if first:
        et0_ref, rel_acc = refs[:2]
        refs = refs[2:]
    elif last:
        stay_ref, leave_ref = refs[:2]
        refs = refs[2:]
    else:
        rel_acc, refs = refs[0], refs[1:]
    lrow_ref, qg_ref, pk = refs[:3]
    old_hbms, refs = refs[3 : 3 + olds], refs[3 + olds :]
    oh_ref, whi_ref, wlo_ref, mult_ref, ops_ref, et_ref, ops_sem, old_sems = refs[:8]
    if last:
        rel_acc, qg_hbm, qg_ref, qg_sem = refs[8], qg_ref, refs[9], refs[10]
    ops_copy = pltpu.make_async_copy(ops_hbm, ops_ref, ops_sem)
    ops_copy.start()
    old_copies = [
        pltpu.make_async_copy(old_refs[n], old_hbms[n], old_sems.at[n]) for n in range(olds)
    ]
    for copy in old_copies:
        copy.start()
    rel_own, width, _ = ops_hbm.shape
    groups = x_ref.shape[0]
    part_rows = slab.shape[0]
    slots = rel_own * 128
    chunk = 256
    chunks = part_rows // chunk
    me = me_ref[0]
    core = me & 1

    lane_row = iota((128, slots), 0)
    lane = iota((128, slots), 1)
    relation, slot = lane >> 7, lane & 7
    per_line = 128 // (8 * rel_own)
    pick_slot = (lane_row == (me % per_line) * (8 * rel_own) + relation * 8 + slot)
    pick_slot = pick_slot.astype(F32).astype(BF)
    count_lane = me * rel_own + relation
    lane = iota((groups, slots), 1)
    own_group = iota((groups, slots), 0) == ((lane >> 3) & (groups - 1))
    slot_row = iota((1, slots), 1) & 7

    def own(values):
        return jnp.sum(jnp.where(own_group, values, 0.0), axis=0, keepdims=True)

    def narrow(values):
        return values.astype(F32).astype(BF)

    s = (0, 1 + core, 2 - core)[turn]
    left, right = x_ref[:, 8 + s, :] >> 16, x_ref[:, 11 + s, :] >> 16
    parts = [left >> 5, left & 31, right >> 5, right & 31]
    parts = dot(narrow(jnp.concatenate(parts, 0)), pick_slot)
    parts = [own(parts[groups * q : groups * (q + 1)]) for q in range(4)]
    left_row = (parts[0] * 32.0 + parts[1]).astype(jnp.int32)
    right_row = (parts[2] * 32.0 + parts[3]).astype(jnp.int32)
    pick_count = narrow(lane_row == count_lane + (s % 2) * (groups * rel_own))
    count_row = own(dot(narrow(x_ref[:, 14 + s // 2, :] >> 16), pick_count))
    live = (count_row.astype(jnp.int32) > slot_row).astype(F32)
    lrow_ref[0:1, :] = left_row

    highs, lows = [], []
    for a in range(8):
        hist = (x_ref[:, (s // 2) * 8 + a, :] >> (16 * (s % 2))) & 65535
        highs.append(hist >> 5)
        lows.append(hist & 31)
        spread_counts(hist.astype(F32), groups, mult_ref, a)
    for q, group in enumerate([highs[:4], highs[4:], lows[:4], lows[4:]]):
        at = width + 16 * q
        pk[at : at + 16, :] = narrow(jnp.concatenate(group, 1))

    slab_t = et0_ref if first else et_ref
    slab_t[...] = slab[...].T

    def left_hot(n, carry):
        at = n * chunk
        oh_ref[pl.ds(at, chunk), :] = one_hot(left_row, n * chunk, (chunk, slots))
        return carry

    def right_hot(n, carry):
        at = n * chunk
        oh_ref[pl.ds(at, chunk), :] = one_hot(right_row, n * chunk, (chunk, slots))
        return carry

    loop(chunks, left_hot, 0)
    left_t = dot(et0_ref[...], oh_ref[...]).astype(BF)
    ops_copy.wait()
    query_t = jnp.concatenate(
        [dot(ops_ref[i], left_t[:, 128 * i : 128 * (i + 1)], TN) for i in range(rel_own)], 1
    ).astype(BF)
    pk[0:width, :] = query_t
    half_t = query_t * 0.5
    loop(chunks, right_hot, 0)
    right_t = dot(slab_t[...], oh_ref[...])
    positive = jnp.sum(query_t.astype(F32) * right_t, axis=0, keepdims=True)
    pos_grad = -live * jax.nn.sigmoid(-positive)
    pos_high = pos_grad.astype(BF)
    pos_low = (pos_grad - pos_high.astype(F32)).astype(BF)
    misc = [narrow(parts[2]), narrow(parts[3]), narrow(live), pos_high, pos_low]
    misc = [row.astype(F32) for row in misc] + [jnp.zeros((11, slots), F32)]
    pk[width + 64 : width + 80, :] = jnp.concatenate(misc, 0).astype(BF)
    factor = live * (0.5 * neg_scale)

    def weigh(n, carry):
        at = n * chunk
        level = jnp.tanh(dot(slab[pl.ds(at, chunk), :], half_t))
        ngrad = (level * factor + factor).astype(BF).astype(F32)
        mult = mult_ref[pl.ds(at, chunk), :]
        weight = ngrad * jnp.concatenate([mult] * rel_own, 1)
        high = weight.astype(BF)
        whi_ref[pl.ds(at, chunk), :] = high
        wlo_ref[pl.ds(at, chunk), :] = (weight - high.astype(F32)).astype(BF)
        return carry

    loop(chunks, weigh, 0)
    qgrad_t = dot(slab_t[...], whi_ref[...]) + dot(slab_t[...], wlo_ref[...])
    qgrad_t = (qgrad_t + right_t * pos_grad).astype(BF)
    qg_ref[...] = qgrad_t
    if last:
        qg_copy = pltpu.make_async_copy(qg_ref, qg_hbm, qg_sem)
        qg_copy.start()
    for i in range(rel_own):
        cols = slice(128 * i, 128 * (i + 1))
        outer = dot(left_t[:, cols], qgrad_t[:, cols], NT)
        rel_acc[i] = outer if first else sum_ref[i] + outer

    for copy in old_copies:
        copy.wait()
    if not last:
        return
    halves, held, _ = stay_ref.shape
    held = held // rel_own
    parity = me_ref[1]
    for ref, owner in ((leave_ref, 1 - parity), (stay_ref, parity)):
        for n in range(halves):
            start = held * (4 * (n >> 1) + 2 * owner + (n & 1))
            rows = pl.ds(pl.multiple_of(start, held), held)
            ref[n] = jnp.concatenate([rel_acc[i, rows, :] for i in range(rel_own)], 0)
    qg_copy.wait()


def right_rows_added(neg_scale, groups, pk, slab_ref, mult_ref, rows_ref, before):
    part_rows, width = slab_ref.shape
    slots = pk.shape[1]
    chunk = 256
    hist = pk[width : width + 64, :].astype(F32)
    hist = hist[:32] * 32.0 + hist[32:]
    for a in range(8):
        cols = slice(128 * (a % 4), 128 * (a % 4 + 1))
        spread_counts(hist[16 * (a // 4) : 16 * (a // 4 + 1), cols], groups, mult_ref, a)
    misc = pk[width + 64 : width + 80, :].astype(F32)
    right_row = (misc[0:1] * 32.0 + misc[1:2]).astype(jnp.int32)
    factor = misc[2:3] * (0.5 * neg_scale)
    pos_grad = misc[3:4] + misc[4:5]
    query_t = pk[0:width, :]
    half_t = query_t * 0.5
    for n in range(part_rows // chunk):
        at = pl.ds(n * chunk, chunk)
        level = jnp.tanh(dot(slab_ref[at, :], half_t))
        ngrad = (level * factor + factor).astype(BF).astype(F32)
        mult = mult_ref[at, :]
        hit = (iota((chunk, slots), 0) + n * chunk) == right_row
        weight = ngrad * jnp.concatenate([mult] * (slots // 128), 1)
        weight = weight + jnp.where(hit, pos_grad, 0.0)
        high = weight.astype(BF)
        low = (weight - high.astype(F32)).astype(BF)
        rows = dot(high, query_t, NT) + dot(low, query_t, NT)
        rows_ref[at, :] = rows if before is None else before[at, :] + rows


def entity_kernel(neg_scale, groups, slab_ref, ops_hbm, *refs):
    lrow_refs, qg_hbms, pk_hbm, pk_other = refs[:3], refs[3:6], refs[6], refs[7]
    rows_ref, mult_ref, ops_ref, qg_ref, pk_ref, sems = refs[8:]
    copies = [
        pltpu.make_async_copy(pk_hbm, pk_ref, sems.at[0]),
        pltpu.make_async_copy(ops_hbm, ops_ref, sems.at[1]),
    ]
    for s in range(3):
        copies.append(pltpu.make_async_copy(qg_hbms[s], qg_ref.at[s], sems.at[2 + s]))
    for copy in copies:
        copy.start()
    rel_own = ops_hbm.shape[0]
    part_rows = slab_ref.shape[0]
    slots = rel_own * 128
    chunk = 256
    right_rows_added(neg_scale, groups, pk_other, slab_ref, mult_ref, rows_ref, None)
    copies[0].wait()
    right_rows_added(neg_scale, groups, pk_ref, slab_ref, mult_ref, rows_ref, rows_ref)
    for copy in copies[1:]:
        copy.wait()
    grads = []
    for s in range(3):
        qgrad_t = qg_ref[s]
        for i in range(rel_own):
            grads.append(dot(ops_ref[i], qgrad_t[:, 128 * i : 128 * (i + 1)]).astype(BF))
    lgrad_t = jnp.concatenate(grads, 1)
    for n in range(part_rows // chunk):
        hot = [one_hot(ref[0:1, :], n * chunk, (chunk, slots)) for ref in lrow_refs]
        rows_ref[pl.ds(n * chunk, chunk), :] += dot(jnp.concatenate(hot, 1), lgrad_t, NT)


def last_entity_kernel(
    neg_scale, groups, me_ref, slab_ref, pk, before, keep_ref, send_ref, rows_ref, mult_ref
):
    right_rows_added(neg_scale, groups, pk, slab_ref, mult_ref, rows_ref, before)
    me = me_ref[0]
    share = slab_ref.shape[0] // groups
    half = groups // 2
    for n in range(groups):
        to = me ^ (((n >> 1) & 3) * 4 + (n & 1) * 2 + (n >> 3))
        block = rows_ref[pl.ds(pl.multiple_of(to * share, share), share), :]
        if n < half:
            keep_ref[n] = block
        else:
            send_ref[n - half] = block


def finish_kernel(keep_ref, got_ref, parts_ref, ent_ref, rel_ref):
    ent_ref[...] = keep_ref[...] + got_ref[...]
    total = parts_ref[0].astype(F32)
    for n in range(1, parts_ref.shape[0]):
        total = total + parts_ref[n].astype(F32)
    rel_ref[...] = total


def shards(entities, operators, left_rows, right_rows, negatives, counts):
    buckets = left_rows.shape[0]
    slot_count = left_rows.shape[-1]
    neg_count = negatives.shape[-1]
    groups = lax.axis_size("span")
    doms = lax.axis_size("dom")
    rel_own = operators.shape[0]
    relations = rel_own * groups
    part_rows, width = entities.shape
    neg_scale = float(neg_count) ** (-0.5)
    share = part_rows // groups
    slots = rel_own * 128
    limit = pltpu.CompilerParams(vmem_limit_bytes=12 * 1024 * 1024)
    small = pltpu.CompilerParams(vmem_limit_bytes=2 * 1024 * 1024)

    packed = pl.pallas_call(
        functools.partial(pack_kernel, groups),
        out_shape=jax.ShapeDtypeStruct((groups, 16, 128), jnp.int32),
        in_specs=[VMEM] * 4,
        out_specs=VMEM,
        name="pack_lists",
    )(
        negatives.reshape(buckets, neg_count // 128, 128),
        left_rows.reshape(buckets, slot_count // 128, 128),
        right_rows.reshape(buckets, slot_count // 128, 128),
        counts.reshape(buckets, 1, relations),
    )
    received = exchanged(packed, "span")
    near = shifted(entities, -1, -2)
    near = pl.pallas_call(
        tie_kernel,
        out_shape=jax.ShapeDtypeStruct(entities.shape, BF),
        in_specs=[VMEM, VMEM],
        out_specs=VMEM,
        compiler_params=small,
        name="after_lists",
    )(near, received)
    slabs = [near, swapped(near, 1)]

    me = jnp.stack([lax.axis_index("span"), (lax.axis_index("dom") >> 1) & 1]).astype(jnp.int32)
    wide = pltpu.VMEM((part_rows, slots), BF)

    packed_shape = (width + 80, slots)
    grad_shape = (width, slots)
    sums = jax.ShapeDtypeStruct((rel_own, width, width), F32)

    def forward(turn, slab, before, olds):
        last = turn == 2
        outs = [jax.ShapeDtypeStruct((width, part_rows), BF)] if turn == 0 else []
        half_sums = jax.ShapeDtypeStruct((doms // 2, rel_own * width // doms, width), F32)
        outs += [half_sums, half_sums] if last else [sums]
        outs.append(jax.ShapeDtypeStruct((8, slots), jnp.int32))
        specs = [VMEM] * len(outs)
        outs.append(pltpu.HBM(grad_shape, BF) if last else jax.ShapeDtypeStruct(grad_shape, BF))
        specs.append(HBM if last else VMEM)
        outs.append(jax.ShapeDtypeStruct(packed_shape, BF))
        specs.append(VMEM)
        outs += [pltpu.HBM(old.shape, BF) for old in olds]
        specs += [HBM] * len(olds)
        scratch = [
            wide,
            wide,
            wide,
            pltpu.VMEM((part_rows, 128), F32),
            pltpu.VMEM(operators.shape, BF),
            pltpu.VMEM((width, part_rows), BF),
            pltpu.SemaphoreType.DMA,
            pltpu.SemaphoreType.DMA((2,)),
        ]
        if last:
            scratch += [
                pltpu.VMEM((rel_own, width, width), F32),
                pltpu.VMEM(grad_shape, BF),
                pltpu.SemaphoreType.DMA,
            ]
        return pl.pallas_call(
            functools.partial(forward_kernel, turn, neg_scale),
            out_shape=outs,
            in_specs=[SMEM, VMEM, VMEM, HBM] + [VMEM] * (len(before) + len(olds)),
            out_specs=specs,
            scratch_shapes=scratch,
            compiler_params=limit,
            cost_estimate=pl.CostEstimate(
                flops=1_450_000_000, bytes_accessed=2_000_000, transcendentals=500_000
            ),
            name=("own_bucket", "near_bucket", "far_bucket")[turn],
        )(me, received, slab, operators, *before, *olds)

    slab_t, rel_sum, lrow_0, qg_0, pack_0 = forward(0, entities, (), ())
    rel_sum, lrow_1, qg_1, pack_1, pack_0, qg_0 = forward(
        1, slabs[0], (slab_t, rel_sum), (pack_0, qg_0)
    )
    pack_1 = shifted(pack_1, 1, 2)
    stay, leave, lrow_2, qg_2, pack_2, qg_1 = forward(2, slabs[1], (slab_t, rel_sum), (qg_1,))
    pack_2 = shifted(pack_2, 2, 1)
    near_pairs = [(d, d ^ 2) for d in range(doms)]
    rel_parts = (stay + lax.ppermute(leave, "dom", near_pairs)).astype(BF)
    alike = [[d for d in range(doms) if (d >> 1) & 1 == parity] for parity in (0, 1)]
    rel_arrived = lax.all_to_all(
        rel_parts, "dom", split_axis=0, concat_axis=0, axis_index_groups=alike, tiled=True
    )

    hold = functools.partial(pltpu.with_memory_space_constraint, memory_space=pltpu.HBM)
    rows = pl.pallas_call(
        functools.partial(entity_kernel, neg_scale, groups),
        out_shape=jax.ShapeDtypeStruct((part_rows, width), F32),
        in_specs=[VMEM, HBM] + [VMEM] * 3 + [HBM] * 4 + [VMEM],
        out_specs=VMEM,
        scratch_shapes=[
            pltpu.VMEM((part_rows, 128), F32),
            pltpu.VMEM(operators.shape, BF),
            pltpu.VMEM((3,) + grad_shape, BF),
            pltpu.VMEM(packed_shape, BF),
            pltpu.SemaphoreType.DMA((5,)),
        ],
        compiler_params=limit,
        cost_estimate=pl.CostEstimate(
            flops=3_000_000_000, bytes_accessed=3_000_000, transcendentals=1_000_000
        ),
        name="entity_gradients",
    )(
        entities,
        operators,
        lrow_0,
        lrow_1,
        lrow_2,
        hold(qg_0),
        hold(qg_1),
        hold(qg_2),
        hold(pack_0),
        pack_1,
    )
    half_parts = jax.ShapeDtypeStruct((groups // 2, share, width), F32)
    keep, send = pl.pallas_call(
        functools.partial(last_entity_kernel, neg_scale, groups),
        out_shape=(half_parts, half_parts),
        in_specs=[SMEM] + [VMEM] * 3,
        out_specs=(VMEM, VMEM),
        scratch_shapes=[
            pltpu.VMEM((part_rows, width), F32),
            pltpu.VMEM((part_rows, 128), F32),
        ],
        compiler_params=limit,
        cost_estimate=pl.CostEstimate(
            flops=1_000_000_000, bytes_accessed=2_000_000, transcendentals=500_000
        ),
        name="last_entity_gradients",
    )(me, entities, pack_2, rows)

    total = keep + swapped(send, 1)
    total = total.reshape(4, 2, share, width)
    got = [swapped(total[x].astype(BF), 4 * x) for x in (1, 2, 3)]
    total = total[0] + sum(part.astype(F32) for part in got)
    held = rel_own * width // doms
    entity_share, rel_share = pl.pallas_call(
        finish_kernel,
        out_shape=(
            jax.ShapeDtypeStruct((share, width), F32),
            jax.ShapeDtypeStruct((held, width), F32),
        ),
        in_specs=[VMEM] * 3,
        out_specs=(VMEM, VMEM),
        compiler_params=small,
        name="last_sums",
    )(total[0], swapped(total[1], 2), rel_arrived)
    return (entity_share, rel_share.reshape(rel_own, width // doms, width))


def solution(mesh):
    in_specs = (
        P("dom", None),
        P("span", None, None),
        P(None, "dom", "span", None),
        P(None, "dom", "span", None),
        P(None, "dom", "span", None),
        P(None, "dom", "span", None),
    )
    out_specs = (P(("dom", "span"), None), P("span", "dom", None))
    return jax.shard_map(shards, mesh=mesh, in_specs=in_specs, out_specs=out_specs, check_vma=False)
```

```python
import functools

import jax
import jax.numpy as jnp
from jax import lax
from jax.experimental import pallas as pl
from jax.experimental.pallas import tpu as pltpu
from jax.sharding import PartitionSpec as P

BF = jnp.bfloat16
F32 = jnp.float32
NT = (((1,), (1,)), ((), ()))
TN = (((0,), (0,)), ((), ()))
VMEM = pl.BlockSpec(memory_space=pltpu.VMEM)
SMEM = pl.BlockSpec(memory_space=pltpu.SMEM)
HBM = pl.BlockSpec(memory_space=pltpu.HBM)


def dot(a, b, dims=(((1,), (0,)), ((), ()))):
    return lax.dot_general(a, b, dims, preferred_element_type=F32)


def shifted(value, step, other):
    doms, groups = lax.axis_size("dom"), lax.axis_size("span")
    pairs = []
    for p in range(doms):
        for c in range(groups):
            to = (p + (other if c & 1 else step)) % doms
            pairs.append((p * groups + c, to * groups + c))
    return lax.ppermute(value, ("dom", "span"), pairs)


def swapped(value, bits):
    groups = lax.axis_size("span")
    return lax.ppermute(value, "span", [(i, i ^ bits) for i in range(groups)])


def exchanged(value, axis):
    return lax.all_to_all(value, axis, split_axis=0, concat_axis=0, tiled=True)


def iota(shape, axis):
    return lax.broadcasted_iota(jnp.int32, shape, axis)


def pack_kernel(groups, neg_ref, left_ref, right_ref, count_ref, out_ref):
    hists = []
    for s in range(3):
        high, low = [], []
        for q in range(neg_ref.shape[1]):
            row = neg_ref[s, q : q + 1, :]
            high.append((iota((16, 128), 0) == (row >> 7)).astype(F32).astype(BF))
            low.append((iota((128, 128), 0) == (row & 127)).astype(F32).astype(BF))
        hist = dot(jnp.concatenate(high, 1), jnp.concatenate(low, 1), NT)[:8]
        hists.append(hist.astype(jnp.int32))
    words = hists[0] + (hists[1] << 16)
    for d in range(groups):
        out_ref[d, 0:8, :] = words
    lines = left_ref.shape[1]
    counts = [count_ref[s] for s in range(3)]
    counts = counts + [jnp.zeros(counts[0].shape, jnp.int32)]
    counts = [jnp.concatenate(counts[:2], 1), jnp.concatenate(counts[2:], 1)]
    for line in range(lines):
        rows = [ref[s, line : line + 1, :] for ref in (left_ref, right_ref) for s in range(3)]
        words = hists[2] + (jnp.concatenate(rows + counts, 0) << 16)
        for d in range(line * groups // lines, (line + 1) * groups // lines):
            out_ref[d, 8:16, :] = words


def loop(n, step, carry):
    for i in range(n):
        carry = step(i, carry)
    return carry


def tie_kernel(held_ref, first_ref, out_ref):
    out_ref[...] = held_ref[...]


def one_hot(rows, at, shape):
    return ((iota(shape, 0) + at) == rows).astype(F32).astype(BF)


def spread_counts(hist, groups, mult_ref, a):
    hist = jnp.broadcast_to(hist[:, None, :], (groups, 8, 128)).reshape(128, 128)
    mult_ref[128 * a : 128 * (a + 1), :] = hist.T


def forward_kernel(turn, neg_scale, *refs):
    first, last = turn == 0, turn == 2
    olds = (0, 2, 1)[turn]
    me_ref, x_ref, slab, ops_hbm = refs[:4]
    refs = refs[4:]
    if not first:
        et0_ref, sum_ref = refs[:2]
        refs = refs[2:]
    old_refs, refs = refs[:olds], refs[olds:]
    if first:
        et0_ref, rel_acc = refs[:2]
        refs = refs[2:]
    elif last:
        rel_ref, refs = refs[0], refs[1:]
    else:
        rel_acc, refs = refs[0], refs[1:]
    lrow_ref, qg_ref, pk = refs[:3]
    old_hbms, refs = refs[3 : 3 + olds], refs[3 + olds :]
    oh_ref, whi_ref, wlo_ref, mult_ref, ops_ref, et_ref, ops_sem, old_sems = refs[:8]
    if last:
        rel_acc, qg_hbm, qg_ref, qg_sem = refs[8], qg_ref, refs[9], refs[10]
    ops_copy = pltpu.make_async_copy(ops_hbm, ops_ref, ops_sem)
    ops_copy.start()
    old_copies = [
        pltpu.make_async_copy(old_refs[n], old_hbms[n], old_sems.at[n]) for n in range(olds)
    ]
    for copy in old_copies:
        copy.start()
    rel_own, width, _ = ops_hbm.shape
    groups = x_ref.shape[0]
    part_rows = slab.shape[0]
    slots = rel_own * 128
    chunk = 256
    chunks = part_rows // chunk
    me = me_ref[0]
    core = me & 1

    lane_row = iota((128, slots), 0)
    lane = iota((128, slots), 1)
    relation, slot = lane >> 7, lane & 7
    per_line = 128 // (8 * rel_own)
    pick_slot = (lane_row == (me % per_line) * (8 * rel_own) + relation * 8 + slot)
    pick_slot = pick_slot.astype(F32).astype(BF)
    count_lane = me * rel_own + relation
    lane = iota((groups, slots), 1)
    own_group = iota((groups, slots), 0) == ((lane >> 3) & (groups - 1))
    slot_row = iota((1, slots), 1) & 7

    def own(values):
        return jnp.sum(jnp.where(own_group, values, 0.0), axis=0, keepdims=True)

    def narrow(values):
        return values.astype(F32).astype(BF)

    s = (0, 1 + core, 2 - core)[turn]
    left, right = x_ref[:, 8 + s, :] >> 16, x_ref[:, 11 + s, :] >> 16
    parts = [left >> 5, left & 31, right >> 5, right & 31]
    parts = dot(narrow(jnp.concatenate(parts, 0)), pick_slot)
    parts = [own(parts[groups * q : groups * (q + 1)]) for q in range(4)]
    left_row = (parts[0] * 32.0 + parts[1]).astype(jnp.int32)
    right_row = (parts[2] * 32.0 + parts[3]).astype(jnp.int32)
    pick_count = narrow(lane_row == count_lane + (s % 2) * (groups * rel_own))
    count_row = own(dot(narrow(x_ref[:, 14 + s // 2, :] >> 16), pick_count))
    live = (count_row.astype(jnp.int32) > slot_row).astype(F32)
    lrow_ref[0:1, :] = left_row

    highs, lows = [], []
    for a in range(8):
        hist = (x_ref[:, (s // 2) * 8 + a, :] >> (16 * (s % 2))) & 65535
        highs.append(hist >> 5)
        lows.append(hist & 31)
        spread_counts(hist.astype(F32), groups, mult_ref, a)
    for q, group in enumerate([highs[:4], highs[4:], lows[:4], lows[4:]]):
        at = width + 16 * q
        pk[at : at + 16, :] = narrow(jnp.concatenate(group, 1))

    slab_t = et0_ref if first else et_ref
    slab_t[...] = slab[...].T

    def left_hot(n, carry):
        at = n * chunk
        oh_ref[pl.ds(at, chunk), :] = one_hot(left_row, n * chunk, (chunk, slots))
        return carry

    def right_hot(n, carry):
        at = n * chunk
        oh_ref[pl.ds(at, chunk), :] = one_hot(right_row, n * chunk, (chunk, slots))
        return carry

    loop(chunks, left_hot, 0)
    left_t = dot(et0_ref[...], oh_ref[...]).astype(BF)
    ops_copy.wait()
    query_t = jnp.concatenate(
        [dot(ops_ref[i], left_t[:, 128 * i : 128 * (i + 1)], TN) for i in range(rel_own)], 1
    ).astype(BF)
    pk[0:width, :] = query_t
    half_t = query_t * 0.5
    loop(chunks, right_hot, 0)
    right_t = dot(slab_t[...], oh_ref[...])
    positive = jnp.sum(query_t.astype(F32) * right_t, axis=0, keepdims=True)
    pos_grad = -live * jax.nn.sigmoid(-positive)
    pos_high = pos_grad.astype(BF)
    pos_low = (pos_grad - pos_high.astype(F32)).astype(BF)
    misc = [narrow(parts[2]), narrow(parts[3]), narrow(live), pos_high, pos_low]
    misc = [row.astype(F32) for row in misc] + [jnp.zeros((11, slots), F32)]
    pk[width + 64 : width + 80, :] = jnp.concatenate(misc, 0).astype(BF)
    factor = live * (0.5 * neg_scale)

    def weigh(n, carry):
        at = n * chunk
        level = jnp.tanh(dot(slab[pl.ds(at, chunk), :], half_t))
        ngrad = (level * factor + factor).astype(BF).astype(F32)
        mult = mult_ref[pl.ds(at, chunk), :]
        weight = ngrad * jnp.concatenate([mult] * rel_own, 1)
        high = weight.astype(BF)
        whi_ref[pl.ds(at, chunk), :] = high
        wlo_ref[pl.ds(at, chunk), :] = (weight - high.astype(F32)).astype(BF)
        return carry

    loop(chunks, weigh, 0)
    qgrad_t = dot(slab_t[...], whi_ref[...]) + dot(slab_t[...], wlo_ref[...])
    qgrad_t = (qgrad_t + right_t * pos_grad).astype(BF)
    qg_ref[...] = qgrad_t
    if last:
        qg_copy = pltpu.make_async_copy(qg_ref, qg_hbm, qg_sem)
        qg_copy.start()
    for i in range(rel_own):
        cols = slice(128 * i, 128 * (i + 1))
        outer = dot(left_t[:, cols], qgrad_t[:, cols], NT)
        rel_acc[i] = outer if first else sum_ref[i] + outer

    for copy in old_copies:
        copy.wait()
    if not last:
        return
    doms, held, _ = rel_ref.shape
    held = held // rel_own
    for d in range(doms):
        block = [rel_acc[i, held * d : held * (d + 1), :] for i in range(rel_own)]
        rel_ref[d] = jnp.concatenate(block, 0).astype(BF)
    qg_copy.wait()


def right_rows_added(neg_scale, groups, pk, slab_ref, mult_ref, rows_ref, before):
    part_rows, width = slab_ref.shape
    slots = pk.shape[1]
    chunk = 256
    hist = pk[width : width + 64, :].astype(F32)
    hist = hist[:32] * 32.0 + hist[32:]
    for a in range(8):
        cols = slice(128 * (a % 4), 128 * (a % 4 + 1))
        spread_counts(hist[16 * (a // 4) : 16 * (a // 4 + 1), cols], groups, mult_ref, a)
    misc = pk[width + 64 : width + 80, :].astype(F32)
    right_row = (misc[0:1] * 32.0 + misc[1:2]).astype(jnp.int32)
    factor = misc[2:3] * (0.5 * neg_scale)
    pos_grad = misc[3:4] + misc[4:5]
    query_t = pk[0:width, :]
    half_t = query_t * 0.5
    for n in range(part_rows // chunk):
        at = pl.ds(n * chunk, chunk)
        level = jnp.tanh(dot(slab_ref[at, :], half_t))
        ngrad = (level * factor + factor).astype(BF).astype(F32)
        mult = mult_ref[at, :]
        hit = (iota((chunk, slots), 0) + n * chunk) == right_row
        weight = ngrad * jnp.concatenate([mult] * (slots // 128), 1)
        weight = weight + jnp.where(hit, pos_grad, 0.0)
        high = weight.astype(BF)
        low = (weight - high.astype(F32)).astype(BF)
        rows = dot(high, query_t, NT) + dot(low, query_t, NT)
        rows_ref[at, :] = rows if before is None else before[at, :] + rows


def entity_kernel(neg_scale, groups, slab_ref, ops_hbm, *refs):
    lrow_refs, qg_hbms, pk_hbm, pk_other = refs[:3], refs[3:6], refs[6], refs[7]
    rows_ref, mult_ref, ops_ref, qg_ref, pk_ref, sems = refs[8:]
    copies = [
        pltpu.make_async_copy(pk_hbm, pk_ref, sems.at[0]),
        pltpu.make_async_copy(ops_hbm, ops_ref, sems.at[1]),
    ]
    for s in range(3):
        copies.append(pltpu.make_async_copy(qg_hbms[s], qg_ref.at[s], sems.at[2 + s]))
    for copy in copies:
        copy.start()
    rel_own = ops_hbm.shape[0]
    part_rows = slab_ref.shape[0]
    slots = rel_own * 128
    chunk = 256
    right_rows_added(neg_scale, groups, pk_other, slab_ref, mult_ref, rows_ref, None)
    copies[0].wait()
    right_rows_added(neg_scale, groups, pk_ref, slab_ref, mult_ref, rows_ref, rows_ref)
    for copy in copies[1:]:
        copy.wait()
    grads = []
    for s in range(3):
        qgrad_t = qg_ref[s]
        for i in range(rel_own):
            grads.append(dot(ops_ref[i], qgrad_t[:, 128 * i : 128 * (i + 1)]).astype(BF))
    lgrad_t = jnp.concatenate(grads, 1)
    for n in range(part_rows // chunk):
        hot = [one_hot(ref[0:1, :], n * chunk, (chunk, slots)) for ref in lrow_refs]
        rows_ref[pl.ds(n * chunk, chunk), :] += dot(jnp.concatenate(hot, 1), lgrad_t, NT)


def last_entity_kernel(
    neg_scale, groups, me_ref, slab_ref, pk, before, keep_ref, send_ref, rows_ref, mult_ref
):
    right_rows_added(neg_scale, groups, pk, slab_ref, mult_ref, rows_ref, before)
    me = me_ref[0]
    share = slab_ref.shape[0] // groups
    half = groups // 2
    for n in range(groups):
        to = me ^ (((n >> 1) & 3) * 4 + (n & 1) * 2 + (n >> 3))
        block = rows_ref[pl.ds(pl.multiple_of(to * share, share), share), :]
        if n < half:
            keep_ref[n] = block
        else:
            send_ref[n - half] = block


def finish_kernel(keep_ref, got_ref, parts_ref, ent_ref, rel_ref):
    ent_ref[...] = keep_ref[...] + got_ref[...]
    total = parts_ref[0].astype(F32)
    for n in range(1, parts_ref.shape[0]):
        total = total + parts_ref[n].astype(F32)
    rel_ref[...] = total


def shards(entities, operators, left_rows, right_rows, negatives, counts):
    buckets = left_rows.shape[0]
    slot_count = left_rows.shape[-1]
    neg_count = negatives.shape[-1]
    groups = lax.axis_size("span")
    doms = lax.axis_size("dom")
    rel_own = operators.shape[0]
    relations = rel_own * groups
    part_rows, width = entities.shape
    neg_scale = float(neg_count) ** (-0.5)
    share = part_rows // groups
    slots = rel_own * 128
    limit = pltpu.CompilerParams(vmem_limit_bytes=12 * 1024 * 1024)
    small = pltpu.CompilerParams(vmem_limit_bytes=2 * 1024 * 1024)

    packed = pl.pallas_call(
        functools.partial(pack_kernel, groups),
        out_shape=jax.ShapeDtypeStruct((groups, 16, 128), jnp.int32),
        in_specs=[VMEM] * 4,
        out_specs=VMEM,
        name="pack_lists",
    )(
        negatives.reshape(buckets, neg_count // 128, 128),
        left_rows.reshape(buckets, slot_count // 128, 128),
        right_rows.reshape(buckets, slot_count // 128, 128),
        counts.reshape(buckets, 1, relations),
    )
    received = exchanged(packed, "span")
    near = shifted(entities, -1, -2)
    near = pl.pallas_call(
        tie_kernel,
        out_shape=jax.ShapeDtypeStruct(entities.shape, BF),
        in_specs=[VMEM, VMEM],
        out_specs=VMEM,
        compiler_params=small,
        name="after_lists",
    )(near, received)
    slabs = [near, swapped(near, 1)]

    me = lax.axis_index("span").astype(jnp.int32).reshape(1)
    wide = pltpu.VMEM((part_rows, slots), BF)

    packed_shape = (width + 80, slots)
    grad_shape = (width, slots)
    sums = jax.ShapeDtypeStruct((rel_own, width, width), F32)

    def forward(turn, slab, before, olds):
        last = turn == 2
        outs = [jax.ShapeDtypeStruct((width, part_rows), BF)] if turn == 0 else []
        relation_parts = jax.ShapeDtypeStruct((doms, rel_own * width // doms, width), BF)
        outs.append(relation_parts if last else sums)
        outs.append(jax.ShapeDtypeStruct((8, slots), jnp.int32))
        specs = [VMEM] * len(outs)
        outs.append(pltpu.HBM(grad_shape, BF) if last else jax.ShapeDtypeStruct(grad_shape, BF))
        specs.append(HBM if last else VMEM)
        outs.append(jax.ShapeDtypeStruct(packed_shape, BF))
        specs.append(VMEM)
        outs += [pltpu.HBM(old.shape, BF) for old in olds]
        specs += [HBM] * len(olds)
        scratch = [
            wide,
            wide,
            wide,
            pltpu.VMEM((part_rows, 128), F32),
            pltpu.VMEM(operators.shape, BF),
            pltpu.VMEM((width, part_rows), BF),
            pltpu.SemaphoreType.DMA,
            pltpu.SemaphoreType.DMA((2,)),
        ]
        if last:
            scratch += [
                pltpu.VMEM((rel_own, width, width), F32),
                pltpu.VMEM(grad_shape, BF),
                pltpu.SemaphoreType.DMA,
            ]
        return pl.pallas_call(
            functools.partial(forward_kernel, turn, neg_scale),
            out_shape=outs,
            in_specs=[SMEM, VMEM, VMEM, HBM] + [VMEM] * (len(before) + len(olds)),
            out_specs=specs,
            scratch_shapes=scratch,
            compiler_params=limit,
            cost_estimate=pl.CostEstimate(
                flops=1_450_000_000, bytes_accessed=2_000_000, transcendentals=500_000
            ),
            name=("own_bucket", "near_bucket", "far_bucket")[turn],
        )(me, received, slab, operators, *before, *olds)

    slab_t, rel_sum, lrow_0, qg_0, pack_0 = forward(0, entities, (), ())
    rel_sum, lrow_1, qg_1, pack_1, pack_0, qg_0 = forward(
        1, slabs[0], (slab_t, rel_sum), (pack_0, qg_0)
    )
    pack_1 = shifted(pack_1, 1, 2)
    rel_parts, lrow_2, qg_2, pack_2, qg_1 = forward(2, slabs[1], (slab_t, rel_sum), (qg_1,))
    pack_2 = shifted(pack_2, 2, 1)
    rel_arrived = exchanged(rel_parts, "dom")

    hold = functools.partial(pltpu.with_memory_space_constraint, memory_space=pltpu.HBM)
    rows = pl.pallas_call(
        functools.partial(entity_kernel, neg_scale, groups),
        out_shape=jax.ShapeDtypeStruct((part_rows, width), F32),
        in_specs=[VMEM, HBM] + [VMEM] * 3 + [HBM] * 4 + [VMEM],
        out_specs=VMEM,
        scratch_shapes=[
            pltpu.VMEM((part_rows, 128), F32),
            pltpu.VMEM(operators.shape, BF),
            pltpu.VMEM((3,) + grad_shape, BF),
            pltpu.VMEM(packed_shape, BF),
            pltpu.SemaphoreType.DMA((5,)),
        ],
        compiler_params=limit,
        cost_estimate=pl.CostEstimate(
            flops=3_000_000_000, bytes_accessed=3_000_000, transcendentals=1_000_000
        ),
        name="entity_gradients",
    )(
        entities,
        operators,
        lrow_0,
        lrow_1,
        lrow_2,
        hold(qg_0),
        hold(qg_1),
        hold(qg_2),
        hold(pack_0),
        pack_1,
    )
    half_parts = jax.ShapeDtypeStruct((groups // 2, share, width), F32)
    keep, send = pl.pallas_call(
        functools.partial(last_entity_kernel, neg_scale, groups),
        out_shape=(half_parts, half_parts),
        in_specs=[SMEM] + [VMEM] * 3,
        out_specs=(VMEM, VMEM),
        scratch_shapes=[
            pltpu.VMEM((part_rows, width), F32),
            pltpu.VMEM((part_rows, 128), F32),
        ],
        compiler_params=limit,
        cost_estimate=pl.CostEstimate(
            flops=1_000_000_000, bytes_accessed=2_000_000, transcendentals=500_000
        ),
        name="last_entity_gradients",
    )(me, entities, pack_2, rows)

    total = keep + swapped(send, 1)
    total = total.reshape(4, 2, share, width)
    got = [swapped(total[x].astype(BF), 4 * x) for x in (2, 1, 3)]
    total = total[0] + sum(part.astype(F32) for part in got)
    held = rel_own * width // doms
    entity_share, rel_share = pl.pallas_call(
        finish_kernel,
        out_shape=(
            jax.ShapeDtypeStruct((share, width), F32),
            jax.ShapeDtypeStruct((held, width), F32),
        ),
        in_specs=[VMEM] * 3,
        out_specs=(VMEM, VMEM),
        compiler_params=small,
        name="last_sums",
    )(total[0], swapped(total[1], 2), rel_arrived)
    return (entity_share, rel_share.reshape(rel_own, width // doms, width))


def solution(mesh):
    in_specs = (
        P("dom", None),
        P("span", None, None),
        P(None, "dom", "span", None),
        P(None, "dom", "span", None),
        P(None, "dom", "span", None),
        P(None, "dom", "span", None),
    )
    out_specs = (P(("dom", "span"), None), P("span", "dom", None))
    return jax.shard_map(shards, mesh=mesh, in_specs=in_specs, out_specs=out_specs, check_vma=False)
```

```python
import functools

import jax
import jax.numpy as jnp
from jax import lax
from jax.experimental import pallas as pl
from jax.experimental.pallas import tpu as pltpu
from jax.sharding import PartitionSpec as P

BF = jnp.bfloat16
F32 = jnp.float32
NT = (((1,), (1,)), ((), ()))
TN = (((0,), (0,)), ((), ()))
VMEM = pl.BlockSpec(memory_space=pltpu.VMEM)
SMEM = pl.BlockSpec(memory_space=pltpu.SMEM)
HBM = pl.BlockSpec(memory_space=pltpu.HBM)


def dot(a, b, dims=(((1,), (0,)), ((), ()))):
    return lax.dot_general(a, b, dims, preferred_element_type=F32)


def shifted(value, step, other):
    doms, groups = lax.axis_size("dom"), lax.axis_size("span")
    pairs = []
    for p in range(doms):
        for c in range(groups):
            to = (p + (other if c & 1 else step)) % doms
            pairs.append((p * groups + c, to * groups + c))
    return lax.ppermute(value, ("dom", "span"), pairs)


def swapped(value, bits):
    groups = lax.axis_size("span")
    return lax.ppermute(value, "span", [(i, i ^ bits) for i in range(groups)])


def exchanged(value, axis):
    return lax.all_to_all(value, axis, split_axis=0, concat_axis=0, tiled=True)


def iota(shape, axis):
    return lax.broadcasted_iota(jnp.int32, shape, axis)


def pack_kernel(groups, neg_ref, left_ref, right_ref, count_ref, out_ref):
    hists = []
    for s in range(3):
        high, low = [], []
        for q in range(neg_ref.shape[1]):
            row = neg_ref[s, q : q + 1, :]
            high.append((iota((16, 128), 0) == (row >> 7)).astype(F32).astype(BF))
            low.append((iota((128, 128), 0) == (row & 127)).astype(F32).astype(BF))
        hist = dot(jnp.concatenate(high, 1), jnp.concatenate(low, 1), NT)[:8]
        hists.append(hist.astype(jnp.int32))
    words = hists[0] + (hists[1] << 16)
    for d in range(groups):
        out_ref[d, 0:8, :] = words
    lines = left_ref.shape[1]
    counts = [count_ref[s] for s in range(3)]
    counts = counts + [jnp.zeros(counts[0].shape, jnp.int32)]
    counts = [jnp.concatenate(counts[:2], 1), jnp.concatenate(counts[2:], 1)]
    for line in range(lines):
        rows = [ref[s, line : line + 1, :] for ref in (left_ref, right_ref) for s in range(3)]
        words = hists[2] + (jnp.concatenate(rows + counts, 0) << 16)
        for d in range(line * groups // lines, (line + 1) * groups // lines):
            out_ref[d, 8:16, :] = words


def loop(n, step, carry):
    for i in range(n):
        carry = step(i, carry)
    return carry


def tie_kernel(held_ref, first_ref, other_ref, out_ref):
    out_ref[...] = held_ref[...]


def turn_kernel(slab_ref, ops_ref, slab_t_ref, ops_t_ref):
    slab_t_ref[...] = slab_ref[...].T
    for i in range(ops_ref.shape[0]):
        ops_t_ref[i] = ops_ref[i].T


def one_hot(rows, at, shape):
    return ((iota(shape, 0) + at) == rows).astype(F32).astype(BF)


def spread_counts(hist, groups, mult_ref, a):
    hist = jnp.broadcast_to(hist[:, None, :], (groups, 8, 128)).reshape(128, 128)
    mult_ref[128 * a : 128 * (a + 1), :] = hist.T


def forward_kernel(turn, neg_scale, *refs):
    first, last = turn == 0, turn == 2
    olds = (0, 2, 1)[turn]
    me_ref, x_ref, slab, ops_ref, et0_ref = refs[:5]
    refs = refs[5:]
    if not first:
        sum_ref, refs = refs[0], refs[1:]
    old_refs, refs = refs[:olds], refs[olds:]
    if last:
        rel_ref, refs = refs[0], refs[1:]
    else:
        rel_acc, refs = refs[0], refs[1:]
    lrow_ref, qg_ref, pk = refs[:3]
    old_hbms, refs = refs[3 : 3 + olds], refs[3 + olds :]
    oh_ref, whi_ref, wlo_ref, mult_ref, et_ref, old_sems = refs[:6]
    if last:
        rel_acc, qg_hbm, qg_ref, qg_sem = refs[6], qg_ref, refs[7], refs[8]
    old_copies = [
        pltpu.make_async_copy(old_refs[n], old_hbms[n], old_sems.at[n]) for n in range(olds)
    ]
    for copy in old_copies:
        copy.start()
    rel_own, width, _ = ops_ref.shape
    groups = x_ref.shape[0]
    part_rows = slab.shape[0]
    slots = rel_own * 128
    chunk = 256
    chunks = part_rows // chunk
    me = me_ref[0]
    core = me & 1

    lane_row = iota((128, slots), 0)
    lane = iota((128, slots), 1)
    relation, slot = lane >> 7, lane & 7
    per_line = 128 // (8 * rel_own)
    pick_slot = (lane_row == (me % per_line) * (8 * rel_own) + relation * 8 + slot)
    pick_slot = pick_slot.astype(F32).astype(BF)
    count_lane = me * rel_own + relation
    lane = iota((groups, slots), 1)
    own_group = iota((groups, slots), 0) == ((lane >> 3) & (groups - 1))
    slot_row = iota((1, slots), 1) & 7

    def own(values):
        return jnp.sum(jnp.where(own_group, values, 0.0), axis=0, keepdims=True)

    def narrow(values):
        return values.astype(F32).astype(BF)

    s = (0, 1 + core, 2 - core)[turn]
    left, right = x_ref[:, 8 + s, :] >> 16, x_ref[:, 11 + s, :] >> 16
    parts = [left >> 5, left & 31, right >> 5, right & 31]
    parts = dot(narrow(jnp.concatenate(parts, 0)), pick_slot)
    parts = [own(parts[groups * q : groups * (q + 1)]) for q in range(4)]
    left_row = (parts[0] * 32.0 + parts[1]).astype(jnp.int32)
    right_row = (parts[2] * 32.0 + parts[3]).astype(jnp.int32)
    pick_count = narrow(lane_row == count_lane + (s % 2) * (groups * rel_own))
    count_row = own(dot(narrow(x_ref[:, 14 + s // 2, :] >> 16), pick_count))
    live = (count_row.astype(jnp.int32) > slot_row).astype(F32)
    lrow_ref[0:1, :] = left_row

    highs, lows = [], []
    for a in range(8):
        hist = (x_ref[:, (s // 2) * 8 + a, :] >> (16 * (s % 2))) & 65535
        highs.append(hist >> 5)
        lows.append(hist & 31)
        spread_counts(hist.astype(F32), groups, mult_ref, a)
    for q, group in enumerate([highs[:4], highs[4:], lows[:4], lows[4:]]):
        at = width + 16 * q
        pk[at : at + 16, :] = narrow(jnp.concatenate(group, 1))

    slab_t = et0_ref if first else et_ref
    if not first:
        slab_t[...] = slab[...].T

    def left_hot(n, carry):
        at = n * chunk
        oh_ref[pl.ds(at, chunk), :] = one_hot(left_row, n * chunk, (chunk, slots))
        return carry

    def right_hot(n, carry):
        at = n * chunk
        oh_ref[pl.ds(at, chunk), :] = one_hot(right_row, n * chunk, (chunk, slots))
        return carry

    loop(chunks, left_hot, 0)
    left_t = dot(et0_ref[...], oh_ref[...]).astype(BF)
    query_t = jnp.concatenate(
        [dot(ops_ref[i], left_t[:, 128 * i : 128 * (i + 1)]) for i in range(rel_own)], 1
    ).astype(BF)
    pk[0:width, :] = query_t
    half_t = query_t * 0.5
    loop(chunks, right_hot, 0)
    right_t = dot(slab_t[...], oh_ref[...])
    positive = jnp.sum(query_t.astype(F32) * right_t, axis=0, keepdims=True)
    pos_grad = -live * jax.nn.sigmoid(-positive)
    pos_high = pos_grad.astype(BF)
    pos_low = (pos_grad - pos_high.astype(F32)).astype(BF)
    misc = [narrow(parts[2]), narrow(parts[3]), narrow(live), pos_high, pos_low]
    misc = [row.astype(F32) for row in misc] + [jnp.zeros((11, slots), F32)]
    pk[width + 64 : width + 80, :] = jnp.concatenate(misc, 0).astype(BF)
    factor = live * (0.5 * neg_scale)

    def weigh(n, carry):
        at = n * chunk
        level = jnp.tanh(dot(slab[pl.ds(at, chunk), :], half_t))
        ngrad = (level * factor + factor).astype(BF).astype(F32)
        mult = mult_ref[pl.ds(at, chunk), :]
        weight = ngrad * jnp.concatenate([mult] * rel_own, 1)
        high = weight.astype(BF)
        whi_ref[pl.ds(at, chunk), :] = high
        wlo_ref[pl.ds(at, chunk), :] = (weight - high.astype(F32)).astype(BF)
        return carry

    loop(chunks, weigh, 0)
    qgrad_t = dot(slab_t[...], whi_ref[...]) + dot(slab_t[...], wlo_ref[...])
    qgrad_t = (qgrad_t + right_t * pos_grad).astype(BF)
    qg_ref[...] = qgrad_t
    if last:
        qg_copy = pltpu.make_async_copy(qg_ref, qg_hbm, qg_sem)
        qg_copy.start()
    for i in range(rel_own):
        cols = slice(128 * i, 128 * (i + 1))
        outer = dot(left_t[:, cols], qgrad_t[:, cols], NT)
        rel_acc[i] = outer if first else sum_ref[i] + outer

    for copy in old_copies:
        copy.wait()
    if not last:
        return
    doms, held, _ = rel_ref.shape
    held = held // rel_own
    for d in range(doms):
        block = [rel_acc[i, held * d : held * (d + 1), :] for i in range(rel_own)]
        rel_ref[d] = jnp.concatenate(block, 0).astype(BF)
    qg_copy.wait()


def right_rows_added(neg_scale, groups, pk, slab_ref, mult_ref, rows_ref, before):
    part_rows, width = slab_ref.shape
    slots = pk.shape[1]
    chunk = 256
    hist = pk[width : width + 64, :].astype(F32)
    hist = hist[:32] * 32.0 + hist[32:]
    for a in range(8):
        cols = slice(128 * (a % 4), 128 * (a % 4 + 1))
        spread_counts(hist[16 * (a // 4) : 16 * (a // 4 + 1), cols], groups, mult_ref, a)
    misc = pk[width + 64 : width + 80, :].astype(F32)
    right_row = (misc[0:1] * 32.0 + misc[1:2]).astype(jnp.int32)
    factor = misc[2:3] * (0.5 * neg_scale)
    pos_grad = misc[3:4] + misc[4:5]
    query_t = pk[0:width, :]
    half_t = query_t * 0.5
    for n in range(part_rows // chunk):
        at = pl.ds(n * chunk, chunk)
        level = jnp.tanh(dot(slab_ref[at, :], half_t))
        ngrad = (level * factor + factor).astype(BF).astype(F32)
        mult = mult_ref[at, :]
        hit = (iota((chunk, slots), 0) + n * chunk) == right_row
        weight = ngrad * jnp.concatenate([mult] * (slots // 128), 1)
        weight = weight + jnp.where(hit, pos_grad, 0.0)
        high = weight.astype(BF)
        low = (weight - high.astype(F32)).astype(BF)
        rows = dot(high, query_t, NT) + dot(low, query_t, NT)
        rows_ref[at, :] = rows if before is None else before[at, :] + rows


def entity_kernel(neg_scale, groups, slab_ref, ops_hbm, *refs):
    lrow_refs, qg_hbms, pk_hbm, pk_other = refs[:3], refs[3:6], refs[6], refs[7]
    rows_ref, mult_ref, ops_ref, qg_ref, pk_ref, sems = refs[8:]
    copies = [
        pltpu.make_async_copy(pk_hbm, pk_ref, sems.at[0]),
        pltpu.make_async_copy(ops_hbm, ops_ref, sems.at[1]),
    ]
    for s in range(3):
        copies.append(pltpu.make_async_copy(qg_hbms[s], qg_ref.at[s], sems.at[2 + s]))
    for copy in copies:
        copy.start()
    rel_own = ops_hbm.shape[0]
    part_rows = slab_ref.shape[0]
    slots = rel_own * 128
    chunk = 256
    right_rows_added(neg_scale, groups, pk_other, slab_ref, mult_ref, rows_ref, None)
    copies[0].wait()
    right_rows_added(neg_scale, groups, pk_ref, slab_ref, mult_ref, rows_ref, rows_ref)
    for copy in copies[1:]:
        copy.wait()
    grads = []
    for s in range(3):
        qgrad_t = qg_ref[s]
        for i in range(rel_own):
            grads.append(dot(ops_ref[i], qgrad_t[:, 128 * i : 128 * (i + 1)]).astype(BF))
    lgrad_t = jnp.concatenate(grads, 1)
    for n in range(part_rows // chunk):
        hot = [one_hot(ref[0:1, :], n * chunk, (chunk, slots)) for ref in lrow_refs]
        rows_ref[pl.ds(n * chunk, chunk), :] += dot(jnp.concatenate(hot, 1), lgrad_t, NT)


def last_entity_kernel(
    neg_scale, groups, me_ref, slab_ref, pk, before, keep_ref, send_ref, rows_ref, mult_ref
):
    right_rows_added(neg_scale, groups, pk, slab_ref, mult_ref, rows_ref, before)
    me = me_ref[0]
    share = slab_ref.shape[0] // groups
    half = groups // 2
    for n in range(groups):
        to = me ^ (((n >> 1) & 3) * 4 + (n & 1) * 2 + (n >> 3))
        block = rows_ref[pl.ds(pl.multiple_of(to * share, share), share), :]
        if n < half:
            keep_ref[n] = block
        else:
            send_ref[n - half] = block


def finish_kernel(keep_ref, got_ref, parts_ref, ent_ref, rel_ref):
    ent_ref[...] = keep_ref[...] + got_ref[...]
    total = parts_ref[0].astype(F32)
    for n in range(1, parts_ref.shape[0]):
        total = total + parts_ref[n].astype(F32)
    rel_ref[...] = total


def shards(entities, operators, left_rows, right_rows, negatives, counts):
    buckets = left_rows.shape[0]
    slot_count = left_rows.shape[-1]
    neg_count = negatives.shape[-1]
    groups = lax.axis_size("span")
    doms = lax.axis_size("dom")
    rel_own = operators.shape[0]
    relations = rel_own * groups
    part_rows, width = entities.shape
    neg_scale = float(neg_count) ** (-0.5)
    share = part_rows // groups
    slots = rel_own * 128
    limit = pltpu.CompilerParams(vmem_limit_bytes=12 * 1024 * 1024)
    small = pltpu.CompilerParams(vmem_limit_bytes=2 * 1024 * 1024)

    packed = pl.pallas_call(
        functools.partial(pack_kernel, groups),
        out_shape=jax.ShapeDtypeStruct((groups, 16, 128), jnp.int32),
        in_specs=[VMEM] * 4,
        out_specs=VMEM,
        name="pack_lists",
    )(
        negatives.reshape(buckets, neg_count // 128, 128),
        left_rows.reshape(buckets, slot_count // 128, 128),
        right_rows.reshape(buckets, slot_count // 128, 128),
        counts.reshape(buckets, 1, relations),
    )
    received = exchanged(packed, "span")
    slab_t, ops_t = pl.pallas_call(
        turn_kernel,
        out_shape=(
            jax.ShapeDtypeStruct((width, part_rows), BF),
            jax.ShapeDtypeStruct(operators.shape, BF),
        ),
        in_specs=[VMEM, VMEM],
        out_specs=(VMEM, VMEM),
        compiler_params=small,
        cost_estimate=pl.CostEstimate(flops=0, bytes_accessed=2_000_000, transcendentals=0),
        name="transposes",
    )(entities, operators)
    near = shifted(entities, -1, -2)
    near = pl.pallas_call(
        tie_kernel,
        out_shape=jax.ShapeDtypeStruct(entities.shape, BF),
        in_specs=[VMEM, VMEM, VMEM],
        out_specs=VMEM,
        compiler_params=small,
        name="after_lists",
    )(near, received, slab_t)
    slabs = [near, swapped(near, 1)]

    me = lax.axis_index("span").astype(jnp.int32).reshape(1)
    wide = pltpu.VMEM((part_rows, slots), BF)

    packed_shape = (width + 80, slots)
    grad_shape = (width, slots)
    sums = jax.ShapeDtypeStruct((rel_own, width, width), F32)

    def forward(turn, slab, before, olds):
        last = turn == 2
        outs = []
        relation_parts = jax.ShapeDtypeStruct((doms, rel_own * width // doms, width), BF)
        outs.append(relation_parts if last else sums)
        outs.append(jax.ShapeDtypeStruct((8, slots), jnp.int32))
        specs = [VMEM] * len(outs)
        outs.append(pltpu.HBM(grad_shape, BF) if last else jax.ShapeDtypeStruct(grad_shape, BF))
        specs.append(HBM if last else VMEM)
        outs.append(jax.ShapeDtypeStruct(packed_shape, BF))
        specs.append(VMEM)
        outs += [pltpu.HBM(old.shape, BF) for old in olds]
        specs += [HBM] * len(olds)
        scratch = [
            wide,
            wide,
            wide,
            pltpu.VMEM((part_rows, 128), F32),
            pltpu.VMEM((width, part_rows), BF),
            pltpu.SemaphoreType.DMA((2,)),
        ]
        if last:
            scratch += [
                pltpu.VMEM((rel_own, width, width), F32),
                pltpu.VMEM(grad_shape, BF),
                pltpu.SemaphoreType.DMA,
            ]
        return pl.pallas_call(
            functools.partial(forward_kernel, turn, neg_scale),
            out_shape=outs,
            in_specs=[SMEM] + [VMEM] * (4 + len(before) + len(olds)),
            out_specs=specs,
            scratch_shapes=scratch,
            compiler_params=limit,
            cost_estimate=pl.CostEstimate(
                flops=1_450_000_000, bytes_accessed=2_000_000, transcendentals=500_000
            ),
            name=("own_bucket", "near_bucket", "far_bucket")[turn],
        )(me, received, slab, ops_t, slab_t, *before, *olds)

    rel_sum, lrow_0, qg_0, pack_0 = forward(0, entities, (), ())
    rel_sum, lrow_1, qg_1, pack_1, pack_0, qg_0 = forward(
        1, slabs[0], (rel_sum,), (pack_0, qg_0)
    )
    pack_1 = shifted(pack_1, 1, 2)
    rel_parts, lrow_2, qg_2, pack_2, qg_1 = forward(2, slabs[1], (rel_sum,), (qg_1,))
    pack_2 = shifted(pack_2, 2, 1)
    rel_arrived = exchanged(rel_parts, "dom")

    hold = functools.partial(pltpu.with_memory_space_constraint, memory_space=pltpu.HBM)
    rows = pl.pallas_call(
        functools.partial(entity_kernel, neg_scale, groups),
        out_shape=jax.ShapeDtypeStruct((part_rows, width), F32),
        in_specs=[VMEM, HBM] + [VMEM] * 3 + [HBM] * 4 + [VMEM],
        out_specs=VMEM,
        scratch_shapes=[
            pltpu.VMEM((part_rows, 128), F32),
            pltpu.VMEM(operators.shape, BF),
            pltpu.VMEM((3,) + grad_shape, BF),
            pltpu.VMEM(packed_shape, BF),
            pltpu.SemaphoreType.DMA((5,)),
        ],
        compiler_params=limit,
        cost_estimate=pl.CostEstimate(
            flops=3_000_000_000, bytes_accessed=3_000_000, transcendentals=1_000_000
        ),
        name="entity_gradients",
    )(
        entities,
        operators,
        lrow_0,
        lrow_1,
        lrow_2,
        hold(qg_0),
        hold(qg_1),
        hold(qg_2),
        hold(pack_0),
        pack_1,
    )
    half_parts = jax.ShapeDtypeStruct((groups // 2, share, width), F32)
    keep, send = pl.pallas_call(
        functools.partial(last_entity_kernel, neg_scale, groups),
        out_shape=(half_parts, half_parts),
        in_specs=[SMEM] + [VMEM] * 3,
        out_specs=(VMEM, VMEM),
        scratch_shapes=[
            pltpu.VMEM((part_rows, width), F32),
            pltpu.VMEM((part_rows, 128), F32),
        ],
        compiler_params=limit,
        cost_estimate=pl.CostEstimate(
            flops=1_000_000_000, bytes_accessed=2_000_000, transcendentals=500_000
        ),
        name="last_entity_gradients",
    )(me, entities, pack_2, rows)

    total = keep + swapped(send, 1)
    total = total.reshape(4, 2, share, width)
    got = [swapped(total[x].astype(BF), 4 * x) for x in (1, 2, 3)]
    total = total[0] + sum(part.astype(F32) for part in got)
    held = rel_own * width // doms
    entity_share, rel_share = pl.pallas_call(
        finish_kernel,
        out_shape=(
            jax.ShapeDtypeStruct((share, width), F32),
            jax.ShapeDtypeStruct((held, width), F32),
        ),
        in_specs=[VMEM] * 3,
        out_specs=(VMEM, VMEM),
        compiler_params=small,
        name="last_sums",
    )(total[0], swapped(total[1], 2), rel_arrived)
    return (entity_share, rel_share.reshape(rel_own, width // doms, width))


def solution(mesh):
    in_specs = (
        P("dom", None),
        P("span", None, None),
        P(None, "dom", "span", None),
        P(None, "dom", "span", None),
        P(None, "dom", "span", None),
        P(None, "dom", "span", None),
    )
    out_specs = (P(("dom", "span"), None), P("span", "dom", None))
    return jax.shard_map(shards, mesh=mesh, in_specs=in_specs, out_specs=out_specs, check_vma=False)
```
